512 devices in a mesh: row: 16 (over z_lo, y), col: 32 (over z_hi, x, core).
Axes of the slice: x: 4, y: 8, z: 8 (z_hi: 4, z_lo: 2; z = z_hi * 2 + z_lo), core: 2. Of those that a mesh axis runs over, the one named last changes fastest.
Arguments:
- inputs: bfloat16 [2560, 6144], P('row', 'col'), may hold values from -48 to 48
- gain: bfloat16 [6144], P('col'), may hold values from 0.5 to 2
- w_in: bfloat16 [6144, 12288], P('row', 'col'), may hold values from -0.15625 to 0.15625
- w_out: bfloat16 [12288, 6144], P('col', 'row'), may hold values from -0.109375 to 0.109375
- grad_out: bfloat16 [2560, 6144], P('row', 'col'), may hold values from -6 to 6
Outputs:
- branch_out: bfloat16 [2560, 6144], P('row', 'col')
- grad_in: bfloat16 [2560, 6144], P('row', 'col')
The draws below stay inside these ranges and needn't reach their ends.
All inputs are finite; a program needn't handle non-finite values.
Results may differ from the reference program's by a relative error of at most 0.02.
Values may be sent and summed in bfloat16 or wider, within the bound.
No kernel may reach another device: no remote copies, remote signals or barrier semaphores. Data moves between devices by JAX's collectives and lax.ppermute only.
A program may use at most 64 MiB of HBM per device.

```python
import math
import jax
import jax.numpy as jnp
from jax import lax

D = 6144
FF = 12288
TOKENS = 2560
N_COL = 32


def draw_inputs(key, part):
    key = jax.random.fold_in(key, 11)
    base_key, column_key, row_key = jax.random.split(key, 3)
    columns = jnp.arange(D, dtype=jnp.float32) / D
    column_scale = jnp.exp(jnp.log(3.0) * columns) * jnp.exp(jax.random.uniform(column_key, (D,), minval=jnp.log(0.33), maxval=0.0))
    row_scale = jnp.exp(jax.random.uniform(row_key, (TOKENS, 1), minval=jnp.log(0.3), maxval=jnp.log(3.0)))
    values = jax.random.normal(base_key, (TOKENS, D)) * column_scale[None, :] * row_scale
    return jnp.clip(values, -48.0, 48.0).astype(jnp.bfloat16)


def spiked(entries, rng, source, target, blocks, factor):
    def block_of(position):
        return (jnp.arange(entries.shape[position]) // (entries.shape[position] // blocks)).reshape((-1,) + (1,) * (entries.ndim - 1 - position))

    one_side = jax.random.permutation(rng, blocks)[block_of(target)]
    far = (block_of(target) + blocks // 2) % blocks
    return jnp.where((block_of(source) == one_side) | (block_of(source) == far), factor * entries, entries)


def level_of(key, shape, cuts, least, largest):
    level, own = 1.0, jax.random.fold_in(key, 6)
    for axis_at, shards_of in cuts:
        steps = jnp.exp(jax.random.uniform(jax.random.fold_in(own, axis_at), (shards_of,), jnp.float32, least / len(cuts), largest / len(cuts)))
        level = level * jnp.repeat(steps, shape[axis_at] // shards_of).reshape([-1 if axis == axis_at else 1 for axis in range(len(shape))])
    return level


def gaussian(stream_key, dims, width, reach, pieces=(), kind=jnp.bfloat16):
    level = level_of(stream_key, dims, pieces, -0.22, 0.18) if pieces else 1.0
    result = jax.random.normal(stream_key, dims, jnp.float32) * width * level
    return jnp.minimum(jnp.maximum(result, -reach), reach).astype(kind)


def heavy_noise(stream_key, extent, scale, most, cuts, heavy, kind=jnp.bfloat16):
    entries = scale * jax.random.normal(stream_key, extent, jnp.float32)
    if cuts:
        entries = entries * level_of(stream_key, extent, cuts, -0.22, 0.18)
    return jnp.clip(spiked(entries, jax.random.fold_in(stream_key, 3), *heavy), -most, most).astype(kind)


def setup_inputs(seed: int = 0) -> dict:
    streams_of = jax.random.split(jax.random.key(seed), 6)
    return {
        "inputs": draw_inputs(jax.random.fold_in(streams_of[5], 71), 0),
        "gain": jnp.clip(jnp.exp(math.log(2.0) - 1.3862944 * jax.random.uniform(streams_of[1], (D,), jnp.float32) ** level_of(streams_of[1], (D,), ((0, 32),), -0.2, 0.2)), 0.5, 2.0).astype(jnp.bfloat16),
        "w_in": heavy_noise(streams_of[2], (D, FF), D ** -0.5, 0.15625, ((0, 16), (1, 32)), (1, 0, 32, 2.75)),
        "w_out": heavy_noise(streams_of[3], (FF, D), FF ** -0.5, 0.109375, ((0, 32), (1, 16)), (0, 1, 32, 2.75)),
        "grad_out": gaussian(streams_of[4], (TOKENS, D), 1.0, 6.0, ((0, 16), (1, 32))),
    }


root_half = 0.7071067811865476
inv_root_tau = 0.3989422804014327
epsilon = 1e-06

def gelu_value(preact):
    return preact * 0.5 * (1.0 + jax.scipy.special.erf(preact * root_half))

def gelu_slope(preact):
    return 0.5 * (1.0 + jax.scipy.special.erf(preact * root_half)) + preact * jnp.exp(-0.5 * preact * preact) * inv_root_tau

def rounded(value):
    narrow = lax.optimization_barrier(value.astype(jnp.bfloat16))
    return narrow.astype(jnp.float32)

def reference(inputs, gain, w_in, w_out, grad_out):
    values = inputs.astype(jnp.float32)
    center = lax.optimization_barrier(jnp.mean(values, axis=1, keepdims=True))
    shifted = values - center
    inverse = lax.rsqrt(lax.optimization_barrier(jnp.mean(shifted * shifted, axis=1, keepdims=True)) + epsilon)
    standard = shifted * inverse
    gain_value = gain.astype(jnp.float32)[None, :]
    normed = (standard * gain_value).astype(jnp.bfloat16)
    preact = jnp.dot(normed, w_in, preferred_element_type=jnp.float32)
    activation = gelu_value(preact).astype(jnp.bfloat16)
    act_grad = jnp.dot(grad_out, w_out.T, preferred_element_type=jnp.float32)
    d_pre = (act_grad * gelu_slope(preact)).astype(jnp.bfloat16)
    block = FF // N_COL
    tokens = inputs.shape[0]

    def accumulate(carry, index):
        out_total, grad_total = carry
        start = (index * block).astype(jnp.int32)
        act_block = lax.dynamic_slice_in_dim(activation, start, block, 1)
        out_rows = lax.dynamic_slice_in_dim(w_out, start, block, 0)
        pre_block = lax.dynamic_slice_in_dim(d_pre, start, block, 1)
        in_cols = lax.dynamic_slice_in_dim(w_in, start, block, 1)
        out_total = out_total + rounded(jnp.dot(act_block, out_rows, preferred_element_type=jnp.float32))
        grad_total = grad_total + rounded(jnp.dot(pre_block, in_cols.T, preferred_element_type=jnp.float32))
        return ((out_total, grad_total), None)
    start_carry = (jnp.zeros((tokens, D), jnp.float32), jnp.zeros((tokens, D), jnp.float32))
    (out_total, d_normed), unused = lax.scan(accumulate, start_carry, jnp.arange(N_COL, dtype=jnp.int32))
    branch_out = out_total.astype(jnp.bfloat16)
    scaled = d_normed * gain_value
    mean_grad = lax.optimization_barrier(jnp.mean(scaled, axis=1, keepdims=True))
    mean_cross = lax.optimization_barrier(jnp.mean(scaled * standard, axis=1, keepdims=True))
    grad_in = inverse * (scaled - mean_grad - standard * mean_cross)
    return (branch_out, grad_in.astype(jnp.bfloat16))
```

```python
import functools

import jax
import jax.numpy as jnp
from jax import lax
from jax.experimental import pallas as pl
from jax.experimental.pallas import tpu as pltpu
from jax.sharding import Mesh
from jax.sharding import PartitionSpec as P

root_half = 0.7071067811865476
inv_root_tau = 0.3989422804014327
epsilon = 1e-06
narrow = jnp.bfloat16
wide = jnp.float32
vmem_bytes = 44 * 2**20


def swap_pairs():
    pairs = []
    for l in range(2):
        for h in range(4):
            pairs.append((l * 4 + h, (h // 2) * 4 + l * 2 + h % 2))
    return pairs


def merge_kernel(core_ref, own0, own1, far0, far1, x_ref, g_ref, gain_ref, stat_ref, mean_s, spread_s):
    step = pl.program_id(0)
    rows = x_ref.shape[1] // 2
    half = x_ref.shape[2] // 2
    block = x_ref.shape[2]
    first = core_ref[0] == 0

    def sides(own, far):
        own, far = own.astype(wide), far.astype(wide)
        a = jnp.where(first, own, far)
        b = jnp.where(first, far, own)
        left = jnp.concatenate([a[:, :half], b[:, :half]], axis=1)
        right = jnp.concatenate([a[:, half:], b[:, half:]], axis=1)
        return left, right

    x0, g0 = sides(own0[0, 0, :rows], far0[0, 0, :rows])
    x1, g1 = sides(own1[0, 0, :rows], far1[0, 0, :rows])
    gain, _ = sides(own0[0, 0, rows:], far0[0, 0, rows:])
    gain_ref[0] = gain
    x_ref[0, :rows] = x0.astype(narrow)
    x_ref[0, rows:] = x1.astype(narrow)
    g_ref[0, :rows] = g0.astype(narrow)
    g_ref[0, rows:] = g1.astype(narrow)

    @pl.when(step == 0)
    def _():
        mean_s[...] = jnp.zeros_like(mean_s)
        spread_s[...] = jnp.zeros_like(spread_s)

    seen = step.astype(wide)
    for index, values in enumerate((x0, x1)):
        at = pl.ds(index * rows, rows)
        center = jnp.sum(values, axis=1, keepdims=True) * (1.0 / block)
        shifted = values - center
        spread = jnp.sum(shifted * shifted, axis=1, keepdims=True)
        gap = center - mean_s[at]
        mean_s[at] = mean_s[at] + gap / (seen + 1.0)
        spread_s[at] = spread_s[at] + spread + gap * gap * (block * seen / (seen + 1.0))

    @pl.when(step == pl.num_programs(0) - 1)
    def _():
        lane = lax.broadcasted_iota(jnp.int32, stat_ref.shape, 1)
        stat_ref[...] = jnp.where(lane < 64, mean_s[...], spread_s[...])


def first_kernel(x_ref, g_ref, gain_ref, stat_ref, panel_ref, sums_ref, pre_s, act_s, gain_s):
    step = pl.program_id(0)
    tokens = x_ref.shape[1]
    block = x_ref.shape[2]

    @pl.when(step == 0)
    def _():
        pre_s[...] = jnp.zeros_like(pre_s)
        act_s[...] = jnp.zeros_like(act_s)
        gain_s[...] = jnp.zeros_like(gain_s)

    w_in = panel_ref[0, :block]
    w_out = panel_ref[0, block:]
    gain = gain_ref[0]
    shifted = ((x_ref[0].astype(wide) - stat_ref[:, :1]) * gain[:1]).astype(narrow)
    pre_s[...] += jnp.dot(shifted, w_in, preferred_element_type=wide)
    act_s[...] += lax.dot_general(
        g_ref[0], w_out, (((1,), (1,)), ((), ())), preferred_element_type=wide
    )
    gain_s[...] += jnp.dot(gain.astype(narrow), w_in, preferred_element_type=wide)

    @pl.when(step == pl.num_programs(0) - 1)
    def _():
        sums_ref[:tokens] = pre_s[...].astype(narrow)
        sums_ref[tokens : 2 * tokens] = act_s[...].astype(narrow)
        high = gain_s[...].astype(narrow).astype(wide)
        sums_ref[2 * tokens :] = jnp.concatenate([high, gain_s[...] - high], axis=0).astype(narrow)


def second_kernel(
    features, core_ref, own_ref, far_ref, stat_ref, far_stat_ref, x_ref, gain_ref, panel_ref,
    keep_ref, send_ref, act_s, pre_s, mean_s, inv_s, flat_s, cross_s,
):
    step = pl.program_id(0)
    tokens = x_ref.shape[1]
    block = x_ref.shape[2]
    rows = tokens // 2
    half = block // 2

    @pl.when(step == 0)
    def _():
        mean_a, mean_b = stat_ref[:, :1], far_stat_ref[:, :1]
        gap = mean_a - mean_b
        mean = 0.5 * (mean_a + mean_b)
        spread = stat_ref[:, 64:65] + far_stat_ref[:, 64:65] + gap * gap * (features / 4)
        inverse = lax.rsqrt(spread / features + epsilon)

        def gain_sum(ref):
            lines = ref[2 * tokens :].astype(wide)
            return lines[:1] + lines[8:9]

        gain_a, gain_b = gain_sum(own_ref), gain_sum(far_ref)
        total = own_ref[:tokens].astype(wide) + far_ref[:tokens].astype(wide)
        total = total + (mean_a - mean) * gain_a + (mean_b - mean) * gain_b
        preact = total * inverse
        act_grad = own_ref[tokens : 2 * tokens].astype(wide) + far_ref[tokens : 2 * tokens].astype(wide)
        bulk = 0.5 * (1.0 + lax.erf(preact * root_half))
        slope = bulk + preact * jnp.exp(-0.5 * preact * preact) * inv_root_tau
        act_s[...] = (preact * bulk).astype(narrow)
        d_pre = (act_grad * slope).astype(narrow)
        pre_s[...] = d_pre
        d_pre = d_pre.astype(wide)
        mean_s[...] = mean
        inv_s[...] = inverse
        flat_s[...] = jnp.sum(d_pre * (gain_a + gain_b), axis=1, keepdims=True) / features
        cross_s[...] = jnp.sum(d_pre * preact, axis=1, keepdims=True) / features

    w_in = panel_ref[0, :block]
    w_out = panel_ref[0, block:]
    out = jnp.dot(act_s[...], w_out, preferred_element_type=wide)
    d_normed = lax.dot_general(
        pre_s[...], w_in, (((1,), (1,)), ((), ())), preferred_element_type=wide
    )
    standard = (x_ref[0].astype(wide) - mean_s[...]) * inv_s[...]
    grad = inv_s[...] * (d_normed * gain_ref[0][:1] - flat_s[...] - standard * cross_s[...])
    side0 = jnp.concatenate([out[:, :half], grad[:, :half]], axis=1)
    side1 = jnp.concatenate([out[:, half:], grad[:, half:]], axis=1)
    first = core_ref[0] == 0
    keep = jnp.where(first, side0, side1).astype(narrow)
    send = jnp.where(first, side1, side0).astype(narrow)
    for index in range(2):
        keep_ref[0, index, 0] = keep[index * rows : (index + 1) * rows]
        send_ref[0, index, 0] = send[index * rows : (index + 1) * rows]


def whole(shape):
    return pl.BlockSpec(shape, lambda j: (0,) * len(shape))


def params():
    return pltpu.CompilerParams(
        dimension_semantics=("arbitrary",), vmem_limit_bytes=vmem_bytes
    )


def on_device(inputs, gain, w_in, w_out, grad_out):
    rows, piece = inputs.shape
    block = 2 * piece
    tokens = 2 * rows
    hidden = w_in.shape[1]
    features = piece * lax.axis_size(("h", "x", "k"))
    steps = features // 2 // block
    other_core = [(0, 1), (1, 0)]
    core = lax.axis_index("k").astype(jnp.int32).reshape(1)

    panels = lax.all_gather(jnp.concatenate([w_in, w_out], axis=0), "y", axis=0)

    gain_rows = jnp.broadcast_to(jnp.concatenate([gain, gain])[None, :], (8, block))
    pack = jnp.concatenate([jnp.concatenate([inputs, grad_out], axis=1), gain_rows], axis=0)
    pack = lax.ppermute(pack, ("l", "h"), swap_pairs())
    pack = lax.all_gather(pack, "h", axis=0)
    own0 = lax.all_gather(pack[:2], "x", axis=0)
    far0 = lax.ppermute(own0, "k", other_core)
    own1 = lax.all_gather(pack[2:], "x", axis=0)
    far1 = lax.ppermute(own1, "k", other_core)

    tile = pl.BlockSpec((1, 1, rows + 8, block), lambda j: (j % 4, j // 4, 0, 0))
    step_block = pl.BlockSpec((1, tokens, block), lambda j: (j, 0, 0))
    gain_block = pl.BlockSpec((1, 8, block), lambda j: (j, 0, 0))
    panel_block = pl.BlockSpec((1,) + panels.shape[1:], lambda j: (j, 0, 0))
    scalar = pl.BlockSpec(memory_space=pltpu.SMEM)
    stat_shape = (tokens, 128)
    column = pltpu.VMEM((tokens, 1), wide)

    values, grads, gains, stats = pl.pallas_call(
        merge_kernel,
        grid=(steps,),
        in_specs=[scalar] + [tile] * 4,
        out_specs=[step_block, step_block, gain_block, whole(stat_shape)],
        out_shape=[
            jax.ShapeDtypeStruct((steps, tokens, block), narrow),
            jax.ShapeDtypeStruct((steps, tokens, block), narrow),
            jax.ShapeDtypeStruct((steps, 8, block), wide),
            jax.ShapeDtypeStruct(stat_shape, wide),
        ],
        scratch_shapes=[column, column],
        compiler_params=params(),
        name="merge",
    )(core, own0, own1, far0, far1)

    sums_shape = (2 * tokens + 16, hidden)
    sums = pl.pallas_call(
        first_kernel,
        grid=(steps,),
        in_specs=[step_block, step_block, gain_block, whole(stat_shape), panel_block],
        out_specs=whole(sums_shape),
        out_shape=jax.ShapeDtypeStruct(sums_shape, narrow),
        scratch_shapes=[
            pltpu.VMEM((tokens, hidden), wide),
            pltpu.VMEM((tokens, hidden), wide),
            pltpu.VMEM((8, hidden), wide),
        ],
        compiler_params=params(),
        name="first",
    )(values, grads, gains, stats, panels)

    far_stats = lax.ppermute(stats, "l", other_core)
    far_sums = lax.ppermute(sums, "l", other_core)

    part_shape = (4, 2, 2, rows, block)
    part_block = pl.BlockSpec((1, 2, 1, rows, block), lambda j: (j % 4, 0, j // 4, 0, 0))
    part = jax.ShapeDtypeStruct(part_shape, narrow)
    keep, send = pl.pallas_call(
        functools.partial(second_kernel, features),
        grid=(steps,),
        in_specs=[
            scalar, whole(sums_shape), whole(sums_shape), whole(stat_shape), whole(stat_shape),
            step_block, gain_block, panel_block,
        ],
        out_specs=[part_block, part_block],
        out_shape=[part, part],
        scratch_shapes=[
            pltpu.VMEM((tokens, hidden), narrow),
            pltpu.VMEM((tokens, hidden), narrow),
            column, column, column, column,
        ],
        compiler_params=params(),
        name="second",
    )(core, sums, far_sums, stats, far_stats, values, gains, panels)

    got = lax.ppermute(send, "k", other_core)
    total = (keep.astype(wide) + got.astype(wide)).astype(narrow)
    total = lax.all_to_all(total, "x", 0, 0)
    total = jnp.sum(total.astype(wide), axis=0).astype(narrow).reshape(4, rows, block)
    total = lax.all_to_all(total, "h", 0, 0)
    total = jnp.sum(total.astype(wide), axis=0).astype(narrow)
    total = lax.ppermute(total, ("l", "h"), swap_pairs())
    return (total[:, :piece], total[:, piece:])


def solution(mesh):
    fine = Mesh(mesh.devices.reshape(2, 8, 4, 4, 2), ("l", "y", "h", "x", "k"))
    row, col = ("l", "y"), ("h", "x", "k")
    in_specs = (P(row, col), P(col), P(row, col), P(col, row), P(row, col))
    out_specs = (P(row, col), P(row, col))
    return jax.shard_map(
        on_device, mesh=fine, in_specs=in_specs, out_specs=out_specs, check_vma=False
    )
```

```python
import functools

import jax
import jax.numpy as jnp
from jax import lax
from jax.experimental import pallas as pl
from jax.experimental.pallas import tpu as pltpu
from jax.sharding import Mesh
from jax.sharding import PartitionSpec as P

root_half = 0.7071067811865476
inv_root_tau = 0.3989422804014327
epsilon = 1e-06
narrow = jnp.bfloat16
wide = jnp.float32


def pairs_of(target):
    pairs = []
    for l in range(2):
        for h in range(4):
            new_l, new_high, new_low = target(l, h // 2, h % 2)
            pairs.append((l * 4 + h, new_l * 4 + new_high * 2 + new_low))
    return pairs


def gather_pairs(i, j):
    return pairs_of(lambda l, high, low: (high, l ^ i, low ^ j))


def scatter_pairs(i, j):
    return pairs_of(lambda l, high, low: (high ^ i, l, low ^ j))


def split3(value):
    high = value.astype(narrow).astype(wide)
    middle = (value - high).astype(narrow).astype(wide)
    return high, middle, value - high - middle


def ones_diagonal(rows, columns):
    row = lax.broadcasted_iota(jnp.int32, (rows, columns), 0)
    column = lax.broadcasted_iota(jnp.int32, (rows, columns), 1)
    return jnp.where(row == column, 1.0, 0.0).astype(narrow)


def merge_kernel(place_ref, own0, own1, far0, far1, x_ref, g_ref, gain_ref, stat_ref, mean_s, spread_s):
    step = pl.program_id(0)
    rows = x_ref.shape[1] // 2
    half = x_ref.shape[2] // 2
    block = x_ref.shape[2]
    first = place_ref[0] == 0

    def sides(own, far):
        own, far = own.astype(wide), far.astype(wide)
        a = jnp.where(first, own, far)
        b = jnp.where(first, far, own)
        left = jnp.concatenate([a[:, :half], b[:, :half]], axis=1)
        right = jnp.concatenate([a[:, half:], b[:, half:]], axis=1)
        return left, right

    x0, g0 = sides(own0[0, 0, :rows], far0[0, 0, :rows])
    x1, g1 = sides(own1[0, 0, :rows], far1[0, 0, :rows])
    gain, _ = sides(own0[0, 0, rows:], far0[0, 0, rows:])
    gain_ref[0] = gain
    x_ref[0, :rows] = x0.astype(narrow)
    x_ref[0, rows:] = x1.astype(narrow)
    g_ref[0, :rows] = g0.astype(narrow)
    g_ref[0, rows:] = g1.astype(narrow)

    @pl.when(step == 0)
    def _():
        mean_s[...] = jnp.zeros_like(mean_s)
        spread_s[...] = jnp.zeros_like(spread_s)

    seen = step.astype(wide)
    for index, values in enumerate((x0, x1)):
        at = pl.ds(index * rows, rows)
        center = jnp.sum(values, axis=1, keepdims=True) * (1.0 / block)
        shifted = values - center
        spread = jnp.sum(shifted * shifted, axis=1, keepdims=True)
        gap = center - mean_s[at]
        mean_s[at] = mean_s[at] + gap / (seen + 1.0)
        spread_s[at] = spread_s[at] + spread + gap * gap * (block * seen / (seen + 1.0))

    @pl.when(step == pl.num_programs(0) - 1)
    def _():
        lane = lax.broadcasted_iota(jnp.int32, stat_ref.shape, 1)
        stat_ref[...] = jnp.where(lane < 64, mean_s[...], spread_s[...])


def first_kernel(place_ref, x_ref, g_ref, gain_ref, stat_ref, panel_ref, sums_ref, pre_s, act_s, gain_s, table_s):
    step = pl.program_id(0)
    tokens = x_ref.shape[1]
    block = x_ref.shape[2]

    @pl.when(step == 0)
    def _():
        pre_s[...] = jnp.zeros_like(pre_s)
        act_s[...] = jnp.zeros_like(act_s)
        gain_s[...] = jnp.zeros_like(gain_s)

    w_in = panel_ref[0, :block]
    w_out = panel_ref[0, block:]
    gain = gain_ref[0]
    shifted = ((x_ref[0].astype(wide) - stat_ref[:, :1]) * gain[:1]).astype(narrow)
    pre_s[...] += jnp.dot(shifted, w_in, preferred_element_type=wide)
    act_s[...] += lax.dot_general(
        g_ref[0], w_out, (((1,), (1,)), ((), ())), preferred_element_type=wide
    )
    gain_s[...] += jnp.dot(gain.astype(narrow), w_in, preferred_element_type=wide)

    @pl.when(step == pl.num_programs(0) - 1)
    def _():
        sums_ref[:tokens] = pre_s[...].astype(narrow)
        sums_ref[tokens : 2 * tokens] = act_s[...].astype(narrow)
        columns = split3(stat_ref[:, :1]) + split3(stat_ref[:, 64:65])
        lane = lax.broadcasted_iota(jnp.int32, (tokens, 128), 1)
        table = jnp.zeros((tokens, 128), wide)
        for index, column in enumerate(columns):
            table = jnp.where(lane == index, column, table)
        table_s[...] = jnp.zeros_like(table_s)
        table_s[:tokens] = table.astype(narrow)
        lines = lax.dot_general(
            ones_diagonal(16, 128), table_s[...], (((1,), (1,)), ((), ())), preferred_element_type=wide
        )
        high = gain_s[:1].astype(narrow).astype(wide)
        row = lax.broadcasted_iota(jnp.int32, lines.shape, 0)
        lines = jnp.where(row == 6, high, jnp.where(row == 7, gain_s[:1] - high, lines))
        sums_ref[2 * tokens :] = lines.astype(narrow)


def second_kernel(
    features, place_ref, own_ref, far_ref, x_ref, gain_ref, panel_ref,
    keep_ref, send_ref, act_s, pre_s, mean_s, inv_s, flat_s, cross_s,
):
    step = pl.program_id(0)
    tokens = x_ref.shape[1]
    block = x_ref.shape[2]
    rows = tokens // 2
    half = block // 2

    @pl.when(step == 0)
    def _():
        def extras(ref):
            lines = ref[2 * tokens :]
            table = lax.dot_general(
                lines, ones_diagonal(16, 128), (((0,), (0,)), ((), ())), preferred_element_type=wide
            )[:tokens]
            center = table[:, 0:1] + table[:, 1:2] + table[:, 2:3]
            spread = table[:, 3:4] + table[:, 4:5] + table[:, 5:6]
            lines = lines.astype(wide)
            return center, spread, lines[6:7] + lines[7:8]

        mean_a, spread_a, gain_a = extras(own_ref)
        mean_b, spread_b, gain_b = extras(far_ref)
        gap = mean_a - mean_b
        mean = 0.5 * (mean_a + mean_b)
        spread = spread_a + spread_b + gap * gap * (features / 4)
        inverse = lax.rsqrt(spread / features + epsilon)

        total = own_ref[:tokens].astype(wide) + far_ref[:tokens].astype(wide)
        total = total + (mean_a - mean) * gain_a + (mean_b - mean) * gain_b
        preact = total * inverse
        act_grad = own_ref[tokens : 2 * tokens].astype(wide) + far_ref[tokens : 2 * tokens].astype(wide)
        bulk = 0.5 * (1.0 + lax.erf(preact * root_half))
        slope = bulk + preact * jnp.exp(-0.5 * preact * preact) * inv_root_tau
        act_s[...] = (preact * bulk).astype(narrow)
        d_pre = (act_grad * slope).astype(narrow)
        pre_s[...] = d_pre
        d_pre = d_pre.astype(wide)
        mean_s[...] = mean
        inv_s[...] = inverse
        flat_s[...] = jnp.sum(d_pre * (gain_a + gain_b), axis=1, keepdims=True) / features
        cross_s[...] = jnp.sum(d_pre * preact, axis=1, keepdims=True) / features

    w_in = panel_ref[0, :block]
    w_out = panel_ref[0, block:]
    out = jnp.dot(act_s[...], w_out, preferred_element_type=wide)
    d_normed = lax.dot_general(
        pre_s[...], w_in, (((1,), (1,)), ((), ())), preferred_element_type=wide
    )
    standard = (x_ref[0].astype(wide) - mean_s[...]) * inv_s[...]
    grad = inv_s[...] * (d_normed * gain_ref[0][:1] - flat_s[...] - standard * cross_s[...])
    out, grad = out.astype(narrow), grad.astype(narrow)
    side0 = jnp.concatenate([out[:, :half], grad[:, :half]], axis=1)
    side1 = jnp.concatenate([out[:, half:], grad[:, half:]], axis=1)
    first = place_ref[0] == 0
    keep = jnp.where(first, side0, side1)
    send = jnp.where(first, side1, side0)
    for index in range(2):
        keep_ref[0, index, 0] = keep[index * rows : (index + 1) * rows]
        send_ref[0, index, 0] = send[index * rows : (index + 1) * rows]


def whole(shape):
    return pl.BlockSpec(shape, lambda j, place: (0,) * len(shape))


def call(kernel, steps, in_specs, out_specs, out_shape, scratch_shapes, vmem, name):
    return pl.pallas_call(
        kernel,
        grid_spec=pltpu.PrefetchScalarGridSpec(
            num_scalar_prefetch=1,
            grid=(steps,),
            in_specs=in_specs,
            out_specs=out_specs,
            scratch_shapes=scratch_shapes,
        ),
        out_shape=out_shape,
        compiler_params=pltpu.CompilerParams(
            dimension_semantics=("arbitrary",), vmem_limit_bytes=vmem * 2**20
        ),
        name=name,
    )


def on_device(inputs, gain, w_in, w_out, grad_out):
    rows, piece = inputs.shape
    block = 2 * piece
    tokens = 2 * rows
    hidden = w_in.shape[1]
    features = piece * lax.axis_size(("h", "x", "k"))
    steps = features // 2 // block
    other_core = [(0, 1), (1, 0)]
    place = jnp.stack([lax.axis_index("k"), lax.axis_index("h") % 2]).astype(jnp.int32)

    panels = lax.all_gather(jnp.concatenate([w_in, w_out], axis=0), "y", axis=0)

    gain_rows = jnp.broadcast_to(jnp.concatenate([gain, gain])[None, :], (8, block))
    pack = jnp.concatenate([jnp.concatenate([inputs, grad_out], axis=1), gain_rows], axis=0)
    near = [
        [lax.ppermute(pack, ("l", "h"), gather_pairs(i, j)) for j in range(2)] for i in range(2)
    ]
    own0 = lax.all_gather(jnp.stack(near[0]), "x", axis=0)
    far0 = lax.ppermute(own0, "k", other_core)
    own1 = lax.all_gather(jnp.stack(near[1]), "x", axis=0)
    far1 = lax.ppermute(own1, "k", other_core)

    tile = pl.BlockSpec((1, 1, rows + 8, block), lambda j, place: (j % 4, j // 4, 0, 0))
    step_block = pl.BlockSpec((1, tokens, block), lambda j, place: (j, 0, 0))
    gain_block = pl.BlockSpec((1, 8, block), lambda j, place: (j, 0, 0))
    panel_block = pl.BlockSpec(
        (1,) + panels.shape[1:], lambda j, place: (((j // 4) ^ place[1]) * 4 + j % 4, 0, 0)
    )
    stat_shape = (tokens, 128)
    column = pltpu.VMEM((tokens, 1), wide)

    values, grads, gains, stats = call(
        merge_kernel,
        steps,
        [tile] * 4,
        [step_block, step_block, gain_block, whole(stat_shape)],
        [
            jax.ShapeDtypeStruct((steps, tokens, block), narrow),
            jax.ShapeDtypeStruct((steps, tokens, block), narrow),
            jax.ShapeDtypeStruct((steps, 8, block), wide),
            jax.ShapeDtypeStruct(stat_shape, wide),
        ],
        [column, column],
        8,
        "merge",
    )(place, own0, own1, far0, far1)

    sums_shape = (2 * tokens + 16, hidden)
    sums = call(
        first_kernel,
        steps,
        [step_block, step_block, gain_block, whole(stat_shape), panel_block],
        whole(sums_shape),
        jax.ShapeDtypeStruct(sums_shape, narrow),
        [
            pltpu.VMEM((tokens, hidden), wide),
            pltpu.VMEM((tokens, hidden), wide),
            pltpu.VMEM((8, hidden), wide),
            pltpu.VMEM((hidden, 128), narrow),
        ],
        12,
        "first",
    )(place, values, grads, gains, stats, panels)

    far_sums = lax.ppermute(sums, "l", other_core)

    part_shape = (4, 2, 2, rows, block)
    part_block = pl.BlockSpec((1, 2, 1, rows, block), lambda j, place: (j % 4, 0, j // 4, 0, 0))
    part = jax.ShapeDtypeStruct(part_shape, narrow)
    keep, send = call(
        functools.partial(second_kernel, features),
        steps,
        [whole(sums_shape), whole(sums_shape), step_block, gain_block, panel_block],
        [part_block, part_block],
        [part, part],
        [
            pltpu.VMEM((tokens, hidden), narrow),
            pltpu.VMEM((tokens, hidden), narrow),
            column, column, column, column,
        ],
        14,
        "second",
    )(place, sums, far_sums, values, gains, panels)

    got = lax.ppermute(send, "k", other_core)
    total = (keep.astype(wide) + got.astype(wide)).astype(narrow)
    total = lax.all_to_all(total, "x", 0, 0)
    total = jnp.sum(total.astype(wide), axis=0).astype(narrow)
    shares = [
        lax.ppermute(total[i, j], ("l", "h"), scatter_pairs(i, j)).astype(wide)
        for i in range(2)
        for j in range(2)
    ]
    total = (shares[0] + shares[1] + shares[2] + shares[3]).astype(narrow)
    return (total[:, :piece], total[:, piece:])


def solution(mesh):
    fine = Mesh(mesh.devices.reshape(2, 8, 4, 4, 2), ("l", "y", "h", "x", "k"))
    row, col = ("l", "y"), ("h", "x", "k")
    in_specs = (P(row, col), P(col), P(row, col), P(col, row), P(row, col))
    out_specs = (P(row, col), P(row, col))
    return jax.shard_map(
        on_device, mesh=fine, in_specs=in_specs, out_specs=out_specs, check_vma=False
    )
```

```python
import functools

import jax
import jax.numpy as jnp
from jax import lax
from jax.experimental import pallas as pl
from jax.experimental.pallas import tpu as pltpu
from jax.sharding import Mesh
from jax.sharding import PartitionSpec as P

root_half = 0.7071067811865476
inv_root_tau = 0.3989422804014327
epsilon = 1e-06
narrow = jnp.bfloat16
wide = jnp.float32


def pairs_of(target):
    pairs = []
    for l in range(2):
        for h in range(4):
            new_l, new_high, new_low = target(l, h // 2, h % 2)
            pairs.append((l * 4 + h, new_l * 4 + new_high * 2 + new_low))
    return pairs


def gather_pairs(i, j):
    return pairs_of(lambda l, high, low: (high, l ^ i, low ^ j))


def scatter_pairs(i, j):
    return pairs_of(lambda l, high, low: (high ^ i, l, low ^ j))


def split3(value):
    high = value.astype(narrow).astype(wide)
    middle = (value - high).astype(narrow).astype(wide)
    return high, middle, value - high - middle


def ones_diagonal(rows, columns):
    row = lax.broadcasted_iota(jnp.int32, (rows, columns), 0)
    column = lax.broadcasted_iota(jnp.int32, (rows, columns), 1)
    return jnp.where(row == column, 1.0, 0.0).astype(narrow)


def stack_kernel(upper, lower, out, sems):
    rows = upper.shape[0]
    copies = [
        pltpu.make_async_copy(upper, out.at[:rows], sems.at[0]),
        pltpu.make_async_copy(lower, out.at[rows:], sems.at[1]),
    ]
    for copy in copies:
        copy.start()
    for copy in copies:
        copy.wait()


def merge_kernel(
    place_ref, own0, own1, far0, far1, x_ref, g_ref, gain_ref, stat_ref, mean_s, gap_s, spread_s
):
    step = pl.program_id(0)
    per_step, tokens, block = x_ref.shape
    rows = tokens // 2
    half = block // 2
    first = place_ref[0] == 0
    ones = jnp.ones((block, 128), narrow)

    def sides(own, far):
        a = jnp.where(first, own, far)
        b = jnp.where(first, far, own)
        left = jnp.concatenate([a[:, :half], b[:, :half]], axis=1)
        right = jnp.concatenate([a[:, half:], b[:, half:]], axis=1)
        return left, right

    @pl.when(step == 0)
    def _():
        mean_s[...] = jnp.zeros_like(mean_s)
        gap_s[...] = jnp.zeros_like(gap_s)
        spread_s[...] = jnp.zeros_like(spread_s)

    for index in range(per_step):
        seen = (step * per_step + index).astype(wide)
        share = 1.0 / (seen + 1.0)
        gain, _ = sides(own0[index, 0, rows:].astype(wide), far0[index, 0, rows:].astype(wide))
        gain_ref[index] = gain
        for part, (own, far) in enumerate(((own0, far0), (own1, far1))):
            at = pl.ds(part * rows, rows)
            values, grads = sides(own[index, 0, :rows], far[index, 0, :rows])
            x_ref[index, at] = values
            g_ref[index, at] = grads
            center = jnp.dot(values, ones, preferred_element_type=wide) * (1.0 / block)
            gap = center - mean_s[at]
            mean_s[at] = mean_s[at] + gap * share
            gap_s[at] = gap_s[at] + gap * gap * (block * seen * share)
            spread = spread_s[at]
            for lane in range(0, block, 128):
                shifted = values[:, lane : lane + 128].astype(wide) - center
                spread = spread + shifted * shifted
            spread_s[at] = spread

    @pl.when(step == pl.num_programs(0) - 1)
    def _():
        lane = lax.broadcasted_iota(jnp.int32, stat_ref.shape, 1)
        spread = jnp.sum(spread_s[...], axis=1, keepdims=True) + gap_s[...]
        stat_ref[...] = jnp.where(lane < 64, mean_s[...], spread)


def first_kernel(place_ref, x_ref, g_ref, gain_ref, stat_ref, panel_ref, sums_ref, pre_s, act_s, gain_s, table_s):
    step = pl.program_id(0)
    per_step, tokens, block = x_ref.shape

    @pl.when(step == 0)
    def _():
        pre_s[...] = jnp.zeros_like(pre_s)
        act_s[...] = jnp.zeros_like(act_s)
        gain_s[...] = jnp.zeros_like(gain_s)

    for index in range(per_step):
        w_in = panel_ref[index, :block]
        w_out = panel_ref[index, block:]
        gain = gain_ref[index]
        shifted = ((x_ref[index].astype(wide) - stat_ref[:, :1]) * gain[:1]).astype(narrow)
        pre_s[...] += jnp.dot(shifted, w_in, preferred_element_type=wide)
        act_s[...] += lax.dot_general(
            g_ref[index], w_out, (((1,), (1,)), ((), ())), preferred_element_type=wide
        )
        gain_s[...] += jnp.dot(gain.astype(narrow), w_in, preferred_element_type=wide)

    @pl.when(step == pl.num_programs(0) - 1)
    def _():
        sums_ref[:tokens] = pre_s[...].astype(narrow)
        sums_ref[tokens : 2 * tokens] = act_s[...].astype(narrow)
        columns = split3(stat_ref[:, :1]) + split3(stat_ref[:, 64:65])
        lane = lax.broadcasted_iota(jnp.int32, (tokens, 128), 1)
        table = jnp.zeros((tokens, 128), wide)
        for index, column in enumerate(columns):
            table = jnp.where(lane == index, column, table)
        table_s[...] = jnp.zeros_like(table_s)
        table_s[:tokens] = table.astype(narrow)
        lines = lax.dot_general(
            ones_diagonal(16, 128), table_s[...], (((1,), (1,)), ((), ())), preferred_element_type=wide
        )
        high = gain_s[:1].astype(narrow).astype(wide)
        row = lax.broadcasted_iota(jnp.int32, lines.shape, 0)
        lines = jnp.where(row == 6, high, jnp.where(row == 7, gain_s[:1] - high, lines))
        sums_ref[2 * tokens :] = lines.astype(narrow)


def second_kernel(
    features, place_ref, own_ref, far_ref, x_ref, gain_ref, panel_ref,
    keep_ref, send_ref, act_s, pre_s, mean_s, inv_s, flat_s, cross_s,
):
    step = pl.program_id(0)
    per_step, tokens, block = x_ref.shape
    rows = tokens // 2
    half = block // 2

    @pl.when(step == 0)
    def _():
        def extras(ref):
            lines = ref[2 * tokens :]
            table = lax.dot_general(
                lines, ones_diagonal(16, 128), (((0,), (0,)), ((), ())), preferred_element_type=wide
            )[:tokens]
            center = table[:, 0:1] + table[:, 1:2] + table[:, 2:3]
            spread = table[:, 3:4] + table[:, 4:5] + table[:, 5:6]
            lines = lines.astype(wide)
            return center, spread, lines[6:7] + lines[7:8]

        mean_a, spread_a, gain_a = extras(own_ref)
        mean_b, spread_b, gain_b = extras(far_ref)
        gap = mean_a - mean_b
        mean = 0.5 * (mean_a + mean_b)
        spread = spread_a + spread_b + gap * gap * (features / 4)
        inverse = lax.rsqrt(spread / features + epsilon)

        total = own_ref[:tokens].astype(wide) + far_ref[:tokens].astype(wide)
        total = total + (mean_a - mean) * gain_a + (mean_b - mean) * gain_b
        preact = total * inverse
        act_grad = own_ref[tokens : 2 * tokens].astype(wide) + far_ref[tokens : 2 * tokens].astype(wide)
        bulk = 0.5 * (1.0 + lax.erf(preact * root_half))
        slope = bulk + preact * jnp.exp(-0.5 * preact * preact) * inv_root_tau
        act_s[...] = (preact * bulk).astype(narrow)
        d_pre = (act_grad * slope).astype(narrow)
        pre_s[...] = d_pre
        d_pre = d_pre.astype(wide)
        mean_s[...] = mean
        inv_s[...] = inverse
        flat_s[...] = jnp.sum(d_pre * (gain_a + gain_b), axis=1, keepdims=True) / features
        cross_s[...] = jnp.sum(d_pre * preact, axis=1, keepdims=True) / features

    first = place_ref[0] == 0
    for index in range(per_step):
        w_in = panel_ref[index, :block]
        w_out = panel_ref[index, block:]
        out = jnp.dot(act_s[...], w_out, preferred_element_type=wide).astype(narrow)
        d_normed = lax.dot_general(
            pre_s[...], w_in, (((1,), (1,)), ((), ())), preferred_element_type=wide
        )
        standard = (x_ref[index].astype(wide) - mean_s[...]) * inv_s[...]
        grad = inv_s[...] * (d_normed * gain_ref[index][:1] - flat_s[...] - standard * cross_s[...])
        grad = grad.astype(narrow)
        side0 = jnp.concatenate([out[:, :half], grad[:, :half]], axis=1)
        side1 = jnp.concatenate([out[:, half:], grad[:, half:]], axis=1)
        keep = jnp.where(first, side0, side1)
        send = jnp.where(first, side1, side0)
        for part in range(2):
            keep_ref[index, part, 0] = keep[part * rows : (part + 1) * rows]
            send_ref[index, part, 0] = send[part * rows : (part + 1) * rows]


def in_hbm(array):
    return pltpu.with_memory_space_constraint(array, pltpu.HBM)


def whole(shape):
    return pl.BlockSpec(shape, lambda j, place: (0,) * len(shape))


def call(kernel, steps, in_specs, out_specs, out_shape, scratch_shapes, vmem, name):
    return pl.pallas_call(
        kernel,
        grid_spec=pltpu.PrefetchScalarGridSpec(
            num_scalar_prefetch=1,
            grid=(steps,),
            in_specs=in_specs,
            out_specs=out_specs,
            scratch_shapes=scratch_shapes,
        ),
        out_shape=out_shape,
        compiler_params=pltpu.CompilerParams(
            dimension_semantics=("arbitrary",), vmem_limit_bytes=vmem * 2**20
        ),
        name=name,
    )


def on_device(inputs, gain, w_in, w_out, grad_out):
    rows, piece = inputs.shape
    block = 2 * piece
    tokens = 2 * rows
    hidden = w_in.shape[1]
    features = piece * lax.axis_size(("h", "x", "k"))
    blocks = features // 2 // block
    steps = blocks // 2
    other_core = [(0, 1), (1, 0)]
    place = jnp.stack([lax.axis_index("k"), lax.axis_index("h") % 2]).astype(jnp.int32)

    weights = pl.pallas_call(
        stack_kernel,
        in_specs=[pl.BlockSpec(memory_space=pl.ANY)] * 2,
        out_specs=pl.BlockSpec(memory_space=pl.ANY),
        out_shape=jax.ShapeDtypeStruct((2 * block, hidden), narrow),
        scratch_shapes=[pltpu.SemaphoreType.DMA((2,))],
        name="stack",
    )(w_in, w_out)
    panels = in_hbm(lax.all_gather(weights, "y", axis=0))

    gain_rows = jnp.broadcast_to(jnp.concatenate([gain, gain])[None, :], (8, block))
    pack = jnp.concatenate([jnp.concatenate([inputs, grad_out], axis=1), gain_rows], axis=0)
    near = [
        [lax.ppermute(pack, ("l", "h"), gather_pairs(i, j)) for j in range(2)] for i in range(2)
    ]
    own0 = lax.all_gather(jnp.stack(near[0]), "x", axis=0)
    far0 = lax.ppermute(own0, "k", other_core)
    own1 = lax.all_gather(jnp.stack(near[1]), "x", axis=0)
    far1 = lax.ppermute(own1, "k", other_core)
    pieces = [in_hbm(piece) for piece in (own0, own1, far0, far1)]

    tile = pl.BlockSpec((2, 1, rows + 8, block), lambda j, place: (j % 2, j // 2, 0, 0))
    step_block = pl.BlockSpec((2, tokens, block), lambda j, place: (j, 0, 0))
    gain_block = pl.BlockSpec((2, 8, block), lambda j, place: (j, 0, 0))
    panel_block = pl.BlockSpec(
        (2,) + panels.shape[1:], lambda j, place: (((j // 2) ^ place[1]) * 2 + j % 2, 0, 0)
    )
    stat_shape = (tokens, 128)
    column = pltpu.VMEM((tokens, 1), wide)

    values, grads, gains, stats = call(
        merge_kernel,
        steps,
        [tile] * 4,
        [step_block, step_block, gain_block, whole(stat_shape)],
        [
            pltpu.HBM((blocks, tokens, block), narrow),
            pltpu.HBM((blocks, tokens, block), narrow),
            pltpu.HBM((blocks, 8, block), wide),
            pltpu.HBM(stat_shape, wide),
        ],
        [pltpu.VMEM(stat_shape, wide)] * 3,
        12,
        "merge",
    )(place, *pieces)

    sums_shape = (2 * tokens + 16, hidden)
    sums = call(
        first_kernel,
        steps,
        [step_block, step_block, gain_block, whole(stat_shape), panel_block],
        whole(sums_shape),
        jax.ShapeDtypeStruct(sums_shape, narrow),
        [
            pltpu.VMEM((tokens, hidden), wide),
            pltpu.VMEM((tokens, hidden), wide),
            pltpu.VMEM((8, hidden), wide),
            pltpu.VMEM((hidden, 128), narrow),
        ],
        12,
        "first",
    )(place, in_hbm(values), in_hbm(grads), gains, stats, panels)

    far_sums = lax.ppermute(sums, "l", other_core)

    part_shape = (4, 2, 2, rows, block)
    part_block = pl.BlockSpec((2, 2, 1, rows, block), lambda j, place: (j % 2, 0, j // 2, 0, 0))
    part = jax.ShapeDtypeStruct(part_shape, narrow)
    keep, send = call(
        functools.partial(second_kernel, features),
        steps,
        [whole(sums_shape), whole(sums_shape), step_block, gain_block, panel_block],
        [part_block, part_block],
        [part, part],
        [
            pltpu.VMEM((tokens, hidden), narrow),
            pltpu.VMEM((tokens, hidden), narrow),
            column, column, column, column,
        ],
        14,
        "second",
    )(place, sums, far_sums, in_hbm(values), gains, panels)

    got = lax.ppermute(send, "k", other_core)
    total = (keep.astype(wide) + got.astype(wide)).astype(narrow)
    total = lax.all_to_all(total, "x", 0, 0)
    total = jnp.sum(total.astype(wide), axis=0).astype(narrow)
    shares = [
        lax.ppermute(total[i, j], ("l", "h"), scatter_pairs(i, j)).astype(wide)
        for i in range(2)
        for j in range(2)
    ]
    total = (shares[0] + shares[1] + shares[2] + shares[3]).astype(narrow)
    return (total[:, :piece], total[:, piece:])


def solution(mesh):
    fine = Mesh(mesh.devices.reshape(2, 8, 4, 4, 2), ("l", "y", "h", "x", "k"))
    row, col = ("l", "y"), ("h", "x", "k")
    in_specs = (P(row, col), P(col), P(row, col), P(col, row), P(row, col))
    out_specs = (P(row, col), P(row, col))
    return jax.shard_map(
        on_device, mesh=fine, in_specs=in_specs, out_specs=out_specs, check_vma=False
    )
```

```python
import functools

import jax
import jax.numpy as jnp
from jax import lax
from jax.experimental import pallas as pl
from jax.experimental.pallas import tpu as pltpu
from jax.sharding import Mesh
from jax.sharding import PartitionSpec as P

root_half = 0.7071067811865476
inv_root_tau = 0.3989422804014327
epsilon = 1e-06
narrow = jnp.bfloat16
wide = jnp.float32


def pairs_of(target):
    pairs = []
    for l in range(2):
        for h in range(4):
            new_l, new_high, new_low = target(l, h // 2, h % 2)
            pairs.append((l * 4 + h, new_l * 4 + new_high * 2 + new_low))
    return pairs


def gather_pairs(i, j):
    return pairs_of(lambda l, high, low: (high, l ^ i, low ^ j))


def scatter_pairs(i, j):
    return pairs_of(lambda l, high, low: (high ^ i, l, low ^ j))


def split3(value):
    high = value.astype(narrow).astype(wide)
    middle = (value - high).astype(narrow).astype(wide)
    return high, middle, value - high - middle


def ones_diagonal(rows, columns):
    row = lax.broadcasted_iota(jnp.int32, (rows, columns), 0)
    column = lax.broadcasted_iota(jnp.int32, (rows, columns), 1)
    return jnp.where(row == column, 1.0, 0.0).astype(narrow)


def halves(a, b):
    lane = lax.broadcasted_iota(jnp.int32, (a.shape[0], 128), 1) < 64
    a0, a1, a2 = (a[:, i : i + 128] for i in (0, 128, 256))
    b0, b1, b2 = (b[:, i : i + 128] for i in (0, 128, 256))
    a1_turned, a2_turned, b0_turned, b1_turned = (
        pltpu.roll(v, 64, 1) for v in (a1, a2, b0, b1)
    )
    left = [a0, jnp.where(lane, a1, b0_turned), jnp.where(lane, b0_turned, b1_turned)]
    right = [jnp.where(lane, a1_turned, a2_turned), jnp.where(lane, a2_turned, b1), b2]
    return left, right


def first_kernel(
    place_ref, own0, own1, far0, far1, panel_ref, x_ref, gain_ref, sums_ref,
    panel_s, sems, g_s, shift_s, table_s,
):
    blocks, rows_in, block = own0.shape[0] * own0.shape[1], own0.shape[2], own0.shape[3]
    tokens = x_ref.shape[0]
    rows, half = tokens // 2, block // 2
    first = place_ref[0] == 0
    flip = place_ref[1]

    def fetch(index):
        at = (index // 4 ^ flip) * 4 + index % 4
        return pltpu.make_async_copy(panel_ref.at[at], panel_s.at[index], sems.at[index])

    for index in range(blocks):
        fetch(index).start()

    def sides(own, far):
        a = jnp.where(first, own, far)
        b = jnp.where(first, far, own)
        left = jnp.concatenate([a[:, :half], b[:, :half]], axis=1)
        right = jnp.concatenate([a[:, half:], b[:, half:]], axis=1)
        return left, right

    means, spreads = [], []
    for part, (own, far) in enumerate(((own0, far0), (own1, far1))):
        at = slice(part * rows, (part + 1) * rows)
        total = jnp.zeros((rows, 128), wide)
        for index in range(blocks):
            x, j = index % 4, index // 4
            to = slice(index * block, (index + 1) * block)
            values, grads = sides(own[x, j, :rows], far[x, j, :rows])
            x_ref[at, to] = values
            g_s[at, to] = grads
            for lane in range(0, block, 128):
                total = total + values[:, lane : lane + 128].astype(wide)
            if part == 0:
                gain_ref[:, to], _ = sides(own[x, j, rows:].astype(wide), far[x, j, rows:].astype(wide))
        mean = jnp.sum(total, axis=1, keepdims=True) * (1.0 / (blocks * block))
        spread = jnp.zeros((rows, 128), wide)
        for lane in range(0, blocks * block, 128):
            shifted = x_ref[at, lane : lane + 128].astype(wide) - mean
            spread = spread + shifted * shifted
            shift_s[at, lane : lane + 128] = (shifted * gain_ref[:1, lane : lane + 128]).astype(narrow)
        means.append(mean)
        spreads.append(jnp.sum(spread, axis=1, keepdims=True))

    pre = act = gain_sum = None
    group = 4
    for start in range(0, blocks, group):
        for index in range(start, start + group):
            fetch(index).wait()
        to = slice(start * block, (start + group) * block)
        w_in = panel_s[start : start + group, :block].reshape(group * block, -1)
        w_out = jnp.concatenate([panel_s[start + i, block:] for i in range(group)], axis=1)
        p = jnp.dot(shift_s[:, to], w_in, preferred_element_type=wide)
        a = lax.dot_general(g_s[:, to], w_out, (((1,), (1,)), ((), ())), preferred_element_type=wide)
        v = jnp.dot(gain_ref[:, to].astype(narrow), w_in, preferred_element_type=wide)
        pre, act, gain_sum = (p, a, v) if pre is None else (pre + p, act + a, gain_sum + v)

    sums_ref[:tokens] = pre.astype(narrow)
    sums_ref[tokens : 2 * tokens] = act.astype(narrow)
    table_s[...] = jnp.zeros_like(table_s)
    for part in range(2):
        columns = split3(means[part]) + split3(spreads[part])
        lane = lax.broadcasted_iota(jnp.int32, (rows, 128), 1)
        table = jnp.zeros((rows, 128), wide)
        for index, column in enumerate(columns):
            table = jnp.where(lane == index, column, table)
        table_s[part * rows : (part + 1) * rows] = table.astype(narrow)
    lines = lax.dot_general(
        ones_diagonal(16, 128), table_s[...], (((1,), (1,)), ((), ())), preferred_element_type=wide
    )
    high = gain_sum[:1].astype(narrow).astype(wide)
    row = lax.broadcasted_iota(jnp.int32, lines.shape, 0)
    lines = jnp.where(row == 6, high, jnp.where(row == 7, gain_sum[:1] - high, lines))
    sums_ref[2 * tokens :] = lines.astype(narrow)


def second_kernel(
    features, place_ref, own_ref, far_ref, x_ref, gain_ref, panel_ref, keep_ref, send_ref
):
    tokens = x_ref.shape[0]
    blocks, block = panel_ref.shape[0], panel_ref.shape[1] // 2
    rows = tokens // 2

    def extras(ref):
        lines = ref[2 * tokens :]
        table = lax.dot_general(
            lines, ones_diagonal(16, 128), (((0,), (0,)), ((), ())), preferred_element_type=wide
        )[:tokens]
        center = table[:, 0:1] + table[:, 1:2] + table[:, 2:3]
        spread = table[:, 3:4] + table[:, 4:5] + table[:, 5:6]
        lines = lines.astype(wide)
        return center, spread, lines[6:7] + lines[7:8]

    mean_a, spread_a, gain_a = extras(own_ref)
    mean_b, spread_b, gain_b = extras(far_ref)
    gap = mean_a - mean_b
    mean = 0.5 * (mean_a + mean_b)
    spread = spread_a + spread_b + gap * gap * (features / 4)
    inverse = lax.rsqrt(spread / features + epsilon)
    total = own_ref[:tokens].astype(wide) + far_ref[:tokens].astype(wide)
    total = total + (mean_a - mean) * gain_a + (mean_b - mean) * gain_b
    preact = total * inverse
    act_grad = own_ref[tokens : 2 * tokens].astype(wide) + far_ref[tokens : 2 * tokens].astype(wide)
    bulk = 0.5 * (1.0 + lax.erf(preact * root_half))
    slope = bulk + preact * jnp.exp(-0.5 * preact * preact) * inv_root_tau
    activation = (preact * bulk).astype(narrow)
    d_pre = (act_grad * slope).astype(narrow)
    d_wide = d_pre.astype(wide)
    flat = inverse * jnp.sum(d_wide * (gain_a + gain_b), axis=1, keepdims=True) / features
    cross = inverse * inverse * jnp.sum(d_wide * preact, axis=1, keepdims=True) / features
    flat = flat - mean * cross

    first = place_ref[0] == 0
    flip = place_ref[1]
    group = 2
    for start in range(0, blocks, group):
        at = (start // 4 ^ flip) * 4 + start % 4
        w_in = panel_ref[pl.ds(at, group), :block].reshape(group * block, -1)
        w_out = jnp.concatenate([panel_ref[at + i, block:] for i in range(group)], axis=1)
        outs = jnp.dot(activation, w_out, preferred_element_type=wide)
        d_normed = lax.dot_general(
            d_pre, w_in, (((1,), (1,)), ((), ())), preferred_element_type=wide
        )
        to = slice(start * block, (start + group) * block)
        grads = inverse * (d_normed * gain_ref[:1, to]) - flat - x_ref[:, to].astype(wide) * cross
        for index in range(start, start + group):
            x, j = index % 4, index // 4
            own = slice((index - start) * block, (index - start + 1) * block)
            sides = halves(outs[:, own], grads[:, own])
            for lane in range(3):
                side0, side1 = (side[lane].astype(narrow) for side in sides)
                keep = jnp.where(first, side0, side1)
                send = jnp.where(first, side1, side0)
                for part in range(2):
                    keep_ref[x, part, j, :, lane * 128 : lane * 128 + 128] = keep[part * rows : (part + 1) * rows]
                    send_ref[x, part, j, :, lane * 128 : lane * 128 + 128] = send[part * rows : (part + 1) * rows]


def in_hbm(array):
    return pltpu.with_memory_space_constraint(array, pltpu.HBM)


def call(kernel, in_specs, out_shape, scratch_shapes, vmem, name):
    here = pl.BlockSpec(memory_space=pltpu.VMEM)
    specs = {"scalar": pl.BlockSpec(memory_space=pltpu.SMEM), "here": here, "any": pl.BlockSpec(memory_space=pl.ANY)}
    return pl.pallas_call(
        kernel,
        in_specs=[specs[spec] for spec in in_specs],
        out_specs=[here] * len(out_shape),
        out_shape=[jax.ShapeDtypeStruct(*shape) for shape in out_shape],
        scratch_shapes=scratch_shapes,
        compiler_params=pltpu.CompilerParams(vmem_limit_bytes=vmem * 2**20),
        name=name,
    )


def first_call(place, own0, own1, far0, far1, panels):
    blocks, twice, hidden = panels.shape
    block, rows = twice // 2, own0.shape[2] - 8
    tokens, width = 2 * rows, blocks * block
    return call(
        first_kernel,
        ["scalar", "here", "here", "here", "here", "any"],
        [((tokens, width), narrow), ((8, width), wide), ((2 * tokens + 16, hidden), narrow)],
        [
            pltpu.VMEM(panels.shape, narrow),
            pltpu.SemaphoreType.DMA((blocks,)),
            pltpu.VMEM((tokens, width), narrow),
            pltpu.VMEM((tokens, width), narrow),
            pltpu.VMEM((hidden, 128), narrow),
        ],
        30,
        "first",
    )(place, own0, own1, far0, far1, panels)


def second_call(features, place, sums, far_sums, values, gains, panels):
    block = panels.shape[1] // 2
    part = ((4, 2, 2, values.shape[0] // 2, block), narrow)
    return call(
        functools.partial(second_kernel, features),
        ["scalar", "here", "here", "here", "here", "here"],
        [part, part],
        [],
        30,
        "second",
    )(place, sums, far_sums, values, gains, panels)


def on_device(inputs, gain, w_in, w_out, grad_out):
    rows, piece = inputs.shape
    block = 2 * piece
    features = piece * lax.axis_size(("h", "x", "k"))
    other_core = [(0, 1), (1, 0)]
    place = jnp.stack([lax.axis_index("k"), lax.axis_index("h") % 2]).astype(jnp.int32)

    panels = lax.all_gather(jnp.concatenate([w_in, w_out], axis=0), "y", axis=0)

    gain_rows = jnp.broadcast_to(jnp.concatenate([gain, gain])[None, :], (8, block))
    pack = jnp.concatenate([jnp.concatenate([inputs, grad_out], axis=1), gain_rows], axis=0)
    near = [
        [lax.ppermute(pack, ("l", "h"), gather_pairs(i, j)) for j in range(2)] for i in range(2)
    ]
    own0 = lax.all_gather(jnp.stack(near[0]), "x", axis=0)
    far0 = lax.ppermute(own0, "k", other_core)
    own1 = lax.all_gather(jnp.stack(near[1]), "x", axis=0)
    far1 = lax.ppermute(own1, "k", other_core)

    values, gains, sums = first_call(place, own0, own1, far0, far1, in_hbm(panels))
    far_sums = lax.ppermute(sums, "l", other_core)
    keep, send = second_call(features, place, sums, far_sums, values, gains, panels)

    got = lax.ppermute(send, "k", other_core)
    total = (keep.astype(wide) + got.astype(wide)).astype(narrow)
    total = lax.all_to_all(total, "x", 0, 0)
    total = jnp.sum(total.astype(wide), axis=0).astype(narrow)
    shares = [
        lax.ppermute(total[i, j], ("l", "h"), scatter_pairs(i, j)).astype(wide)
        for i in range(2)
        for j in range(2)
    ]
    total = (shares[0] + shares[1] + shares[2] + shares[3]).astype(narrow)
    return (total[:, :piece], total[:, piece:])


def solution(mesh):
    fine = Mesh(mesh.devices.reshape(2, 8, 4, 4, 2), ("l", "y", "h", "x", "k"))
    row, col = ("l", "y"), ("h", "x", "k")
    in_specs = (P(row, col), P(col), P(row, col), P(col, row), P(row, col))
    out_specs = (P(row, col), P(row, col))
    return jax.shard_map(
        on_device, mesh=fine, in_specs=in_specs, out_specs=out_specs, check_vma=False
    )
```

```python
import functools

import jax
import jax.numpy as jnp
from jax import lax
from jax.experimental import pallas as pl
from jax.experimental.pallas import tpu as pltpu
from jax.sharding import Mesh
from jax.sharding import PartitionSpec as P

root_half = 0.7071067811865476
inv_root_tau = 0.3989422804014327
epsilon = 1e-06
narrow = jnp.bfloat16
wide = jnp.float32


def pairs_of(target):
    pairs = []
    for l in range(2):
        for h in range(4):
            new_l, new_high, new_low = target(l, h // 2, h % 2)
            pairs.append((l * 4 + h, new_l * 4 + new_high * 2 + new_low))
    return pairs


def gather_pairs(i, j):
    return pairs_of(lambda l, high, low: (high, l ^ i, low ^ j))


def scatter_pairs(i, j):
    return pairs_of(lambda l, high, low: (high ^ i, l, low ^ j))


def split3(value):
    high = value.astype(narrow).astype(wide)
    middle = (value - high).astype(narrow).astype(wide)
    return high, middle, value - high - middle


def ones_diagonal(rows, columns):
    row = lax.broadcasted_iota(jnp.int32, (rows, columns), 0)
    column = lax.broadcasted_iota(jnp.int32, (rows, columns), 1)
    return jnp.where(row == column, 1.0, 0.0).astype(narrow)


def halves(a, b):
    lane = lax.broadcasted_iota(jnp.int32, (a.shape[0], 128), 1) < 64
    a0, a1, a2 = (a[:, i : i + 128] for i in (0, 128, 256))
    b0, b1, b2 = (b[:, i : i + 128] for i in (0, 128, 256))
    a1_turned, a2_turned, b0_turned, b1_turned = (
        pltpu.roll(v, 64, 1) for v in (a1, a2, b0, b1)
    )
    left = [a0, jnp.where(lane, a1, b0_turned), jnp.where(lane, b0_turned, b1_turned)]
    right = [jnp.where(lane, a1_turned, a2_turned), jnp.where(lane, a2_turned, b1), b2]
    return left, right


def merge_kernel(
    place_ref, own0, own1, far0, far1, x_ref, shift_ref, g_ref, gain_ref, table_ref
):
    blocks, block = own0.shape[0] * own0.shape[1], own0.shape[3]
    tokens = x_ref.shape[0]
    rows, half = tokens // 2, block // 2
    first = place_ref[0] == 0

    def sides(own, far):
        a = jnp.where(first, own, far)
        b = jnp.where(first, far, own)
        left = jnp.concatenate([a[:, :half], b[:, :half]], axis=1)
        right = jnp.concatenate([a[:, half:], b[:, half:]], axis=1)
        return left, right

    table_ref[...] = jnp.zeros_like(table_ref)
    for part, (own, far) in enumerate(((own0, far0), (own1, far1))):
        at = slice(part * rows, (part + 1) * rows)
        total = jnp.zeros((rows, 128), wide)
        for index in range(blocks):
            x, j = index % 4, index // 4
            to = slice(index * block, (index + 1) * block)
            values, grads = sides(own[x, j, :rows], far[x, j, :rows])
            x_ref[at, to] = values
            wide_to = slice(index % 2 * block, (index % 2 + 1) * block)
            g_ref[index // 2, at, wide_to] = grads
            for lane in range(0, block, 128):
                total = total + values[:, lane : lane + 128].astype(wide)
            if part == 0:
                gain_ref[:, to], _ = sides(own[x, j, rows:].astype(wide), far[x, j, rows:].astype(wide))
        mean = jnp.sum(total, axis=1, keepdims=True) * (1.0 / (blocks * block))
        spread = jnp.zeros((rows, 128), wide)
        for lane in range(0, blocks * block, 128):
            shifted = x_ref[at, lane : lane + 128].astype(wide) - mean
            spread = spread + shifted * shifted
            pair, to = lane // (2 * block), lane % (2 * block)
            shift_ref[pair, at, to : to + 128] = (shifted * gain_ref[:1, lane : lane + 128]).astype(narrow)
        columns = split3(mean) + split3(jnp.sum(spread, axis=1, keepdims=True))
        lane = lax.broadcasted_iota(jnp.int32, (rows, 128), 1)
        table = jnp.zeros((rows, 128), wide)
        for index, column in enumerate(columns):
            table = jnp.where(lane == index, column, table)
        table_ref[at] = table.astype(narrow)


def first_kernel(
    place_ref, gain_ref, table_ref, shift_ref, g_ref, panel_ref, sums_ref,
    shift_s, g_s, panel_s, sems,
):
    pairs, tokens, width = shift_ref.shape
    block = width // 2
    flip = place_ref[1]

    def fetch(pair):
        at = (pair // 2 ^ flip) * 2 + pair % 2
        moves = (
            (shift_ref.at[pair], shift_s.at[pair]),
            (g_ref.at[pair], g_s.at[pair]),
            (panel_ref.at[pl.ds(at * 2, 2)], panel_s.at[pair]),
        )
        return [
            pltpu.make_async_copy(source, target, sems.at[pair, i])
            for i, (source, target) in enumerate(moves)
        ]

    for pair in range(pairs):
        for copy in fetch(pair):
            copy.start()

    pre = act = gain_sum = None
    for pair in range(pairs):
        for copy in fetch(pair):
            copy.wait()
        to = slice(pair * width, (pair + 1) * width)
        w_in = panel_s[pair, :, :block].reshape(width, -1)
        w_out = jnp.concatenate([panel_s[pair, i, block:] for i in range(2)], axis=1)
        p = jnp.dot(shift_s[pair], w_in, preferred_element_type=wide)
        a = lax.dot_general(g_s[pair], w_out, (((1,), (1,)), ((), ())), preferred_element_type=wide)
        v = jnp.dot(gain_ref[:, to].astype(narrow), w_in, preferred_element_type=wide)
        pre, act, gain_sum = (p, a, v) if pre is None else (pre + p, act + a, gain_sum + v)

    sums_ref[:tokens] = pre.astype(narrow)
    sums_ref[tokens : 2 * tokens] = act.astype(narrow)
    lines = lax.dot_general(
        ones_diagonal(16, 128), table_ref[...], (((1,), (1,)), ((), ())), preferred_element_type=wide
    )
    high = gain_sum[:1].astype(narrow).astype(wide)
    row = lax.broadcasted_iota(jnp.int32, lines.shape, 0)
    lines = jnp.where(row == 6, high, jnp.where(row == 7, gain_sum[:1] - high, lines))
    sums_ref[2 * tokens :] = lines.astype(narrow)


def second_kernel(
    features, place_ref, own_ref, far_ref, x_ref, gain_ref, panel_ref, *out_refs
):
    tokens = x_ref.shape[0]
    blocks, block = panel_ref.shape[0], panel_ref.shape[1] // 2
    rows = tokens // 2

    def extras(ref):
        lines = ref[2 * tokens :]
        table = lax.dot_general(
            lines, ones_diagonal(16, 128), (((0,), (0,)), ((), ())), preferred_element_type=wide
        )[:tokens]
        center = table[:, 0:1] + table[:, 1:2] + table[:, 2:3]
        spread = table[:, 3:4] + table[:, 4:5] + table[:, 5:6]
        lines = lines.astype(wide)
        return center, spread, lines[6:7] + lines[7:8]

    mean_a, spread_a, gain_a = extras(own_ref)
    mean_b, spread_b, gain_b = extras(far_ref)
    gap = mean_a - mean_b
    mean = 0.5 * (mean_a + mean_b)
    spread = spread_a + spread_b + gap * gap * (features / 4)
    inverse = lax.rsqrt(spread / features + epsilon)
    total = own_ref[:tokens].astype(wide) + far_ref[:tokens].astype(wide)
    total = total + (mean_a - mean) * gain_a + (mean_b - mean) * gain_b
    preact = total * inverse
    act_grad = own_ref[tokens : 2 * tokens].astype(wide) + far_ref[tokens : 2 * tokens].astype(wide)
    bulk = 0.5 * (1.0 + lax.erf(preact * root_half))
    slope = bulk + preact * jnp.exp(-0.5 * preact * preact) * inv_root_tau
    activation = (preact * bulk).astype(narrow)
    d_pre = (act_grad * slope).astype(narrow)
    d_wide = d_pre.astype(wide)
    flat = inverse * jnp.sum(d_wide * (gain_a + gain_b), axis=1, keepdims=True) / features
    cross = inverse * inverse * jnp.sum(d_wide * preact, axis=1, keepdims=True) / features
    flat = flat - mean * cross

    first = place_ref[0] == 0
    flip = place_ref[1]
    group = 2
    for start in range(0, blocks, group):
        at = (start // 4 ^ flip) * 4 + start % 4
        w_in = panel_ref[pl.ds(at, group), :block].reshape(group * block, -1)
        w_out = jnp.concatenate([panel_ref[at + i, block:] for i in range(group)], axis=1)
        outs = jnp.dot(activation, w_out, preferred_element_type=wide)
        d_normed = lax.dot_general(
            d_pre, w_in, (((1,), (1,)), ((), ())), preferred_element_type=wide
        )
        to = slice(start * block, (start + group) * block)
        grads = inverse * (d_normed * gain_ref[:1, to]) - flat - x_ref[:, to].astype(wide) * cross
        for index in range(start, start + group):
            x, j = index % 4, index // 4
            own = slice((index - start) * block, (index - start + 1) * block)
            sides = halves(outs[:, own], grads[:, own])
            for lane in range(3):
                side0, side1 = (side[lane].astype(narrow) for side in sides)
                keep = jnp.where(first, side0, side1)
                send = jnp.where(first, side1, side0)
                to = slice(lane * 128, lane * 128 + 128)
                for part in range(2):
                    at = slice(part * rows, (part + 1) * rows)
                    target = x if part == 0 else (x - place_ref[2]) & 3
                    out_refs[part][target, j, :, to] = keep[at]
                    out_refs[2 + part][target, j, :, to] = send[at]


def in_hbm(array):
    return pltpu.with_memory_space_constraint(array, pltpu.HBM)


def call(kernel, in_specs, out_shape, scratch_shapes, vmem, name):
    here = pl.BlockSpec(memory_space=pltpu.VMEM)
    specs = {"scalar": pl.BlockSpec(memory_space=pltpu.SMEM), "here": here, "any": pl.BlockSpec(memory_space=pl.ANY)}
    return pl.pallas_call(
        kernel,
        in_specs=[specs[spec] for spec in in_specs],
        out_specs=[here] * len(out_shape),
        out_shape=out_shape,
        scratch_shapes=scratch_shapes,
        compiler_params=pltpu.CompilerParams(vmem_limit_bytes=vmem * 2**20),
        name=name,
    )


def merge_call(place, own0, own1, far0, far1, hidden):
    blocks, block = own0.shape[0] * own0.shape[1], own0.shape[3]
    tokens, width = 2 * (own0.shape[2] - 8), blocks * block
    return call(
        merge_kernel,
        ["scalar", "here", "here", "here", "here"],
        [
            pltpu.HBM((tokens, width), narrow),
            pltpu.HBM((blocks // 2, tokens, 2 * block), narrow),
            pltpu.HBM((blocks // 2, tokens, 2 * block), narrow),
            jax.ShapeDtypeStruct((8, width), wide),
            jax.ShapeDtypeStruct((hidden, 128), narrow),
        ],
        [],
        30,
        "merge",
    )(place, own0, own1, far0, far1)


def first_call(place, shifted, grads, gains, table, panels):
    blocks, twice, hidden = panels.shape
    pairs, tokens, width = shifted.shape
    (sums,) = call(
        first_kernel,
        ["scalar", "here", "here", "any", "any", "any"],
        [jax.ShapeDtypeStruct((2 * tokens + 16, hidden), narrow)],
        [
            pltpu.VMEM(shifted.shape, narrow),
            pltpu.VMEM(grads.shape, narrow),
            pltpu.VMEM((pairs, blocks // pairs, twice, hidden), narrow),
            pltpu.SemaphoreType.DMA((pairs, 3)),
        ],
        30,
        "first",
    )(place, gains, table, in_hbm(shifted), in_hbm(grads), in_hbm(panels))
    return sums


def second_call(features, place, sums, far_sums, values, gains, panels):
    block = panels.shape[1] // 2
    part = jax.ShapeDtypeStruct((4, 2, values.shape[0] // 2, block), narrow)
    return call(
        functools.partial(second_kernel, features),
        ["scalar", "here", "here", "here", "here", "here"],
        [part] * 4,
        [],
        30,
        "second",
    )(place, sums, far_sums, values, gains, panels)


def on_device(inputs, gain, w_in, w_out, grad_out):
    rows, piece = inputs.shape
    block = 2 * piece
    features = piece * lax.axis_size(("h", "x", "k"))
    other_core = [(0, 1), (1, 0)]
    place = jnp.stack([lax.axis_index("k"), lax.axis_index("h") % 2, lax.axis_index("x")]).astype(jnp.int32)

    panels = lax.all_gather(jnp.concatenate([w_in, w_out], axis=0), "y", axis=0)

    gain_rows = jnp.broadcast_to(jnp.concatenate([gain, gain])[None, :], (8, block))
    pack = jnp.concatenate([jnp.concatenate([inputs, grad_out], axis=1), gain_rows], axis=0)
    near = [
        [lax.ppermute(pack, ("l", "h"), gather_pairs(i, j)) for j in range(2)] for i in range(2)
    ]
    own0 = lax.all_gather(jnp.stack(near[0]), "x", axis=0)
    far0 = lax.ppermute(own0, "k", other_core)
    own1 = lax.all_gather(jnp.stack(near[1]), "x", axis=0)
    far1 = lax.ppermute(own1, "k", other_core)

    values, shifted, grads, gains, table = merge_call(place, own0, own1, far0, far1, w_in.shape[1])
    sums = first_call(place, shifted, grads, gains, table, panels)
    far_sums = lax.ppermute(sums, "l", other_core)
    outs = second_call(features, place, sums, far_sums, values, gains, panels)

    got = [lax.ppermute(send, "k", other_core) for send in outs[2:]]
    def add(a, b):
        return (a.astype(wide) + b.astype(wide)).astype(narrow)

    first = lax.all_to_all(add(outs[0], got[0]), "x", 0, 0)
    second = [add(outs[1][d], got[1][d]) for d in range(4)]
    second = [second[0]] + [
        lax.ppermute(second[d], "x", [(x, (x + d) % 4) for x in range(4)]) for d in (1, 3, 2)
    ]
    shares = []
    for i, parts in enumerate(([first[x] for x in range(4)], second)):
        part = sum(part.astype(wide) for part in parts).astype(narrow)
        shares += [lax.ppermute(part[j], ("l", "h"), scatter_pairs(i, j)).astype(wide) for j in range(2)]
    total = (shares[0] + shares[1] + shares[2] + shares[3]).astype(narrow)
    return (total[:, :piece], total[:, piece:])


def solution(mesh):
    fine = Mesh(mesh.devices.reshape(2, 8, 4, 4, 2), ("l", "y", "h", "x", "k"))
    row, col = ("l", "y"), ("h", "x", "k")
    in_specs = (P(row, col), P(col), P(row, col), P(col, row), P(row, col))
    out_specs = (P(row, col), P(row, col))
    return jax.shard_map(
        on_device, mesh=fine, in_specs=in_specs, out_specs=out_specs, check_vma=False
    )
```

```python
import functools

import jax
import jax.numpy as jnp
from jax import lax
from jax.experimental import pallas as pl
from jax.experimental.pallas import tpu as pltpu
from jax.sharding import Mesh
from jax.sharding import PartitionSpec as P

root_half = 0.7071067811865476
inv_root_tau = 0.3989422804014327
epsilon = 1e-06
narrow = jnp.bfloat16
wide = jnp.float32
relative = (True, True)


def pairs_of(target):
    pairs = []
    for l in range(2):
        for h in range(4):
            new_l, new_high, new_low = target(l, h // 2, h % 2)
            pairs.append((l * 4 + h, new_l * 4 + new_high * 2 + new_low))
    return pairs


def gather_pairs(i, j):
    return pairs_of(lambda l, high, low: (high, l ^ i, low ^ j))


def scatter_pairs(i, j):
    return pairs_of(lambda l, high, low: (high ^ i, l, low ^ j))


def split3(value):
    high = value.astype(narrow).astype(wide)
    middle = (value - high).astype(narrow).astype(wide)
    return high, middle, value - high - middle


def ones_diagonal(rows, columns):
    row = lax.broadcasted_iota(jnp.int32, (rows, columns), 0)
    column = lax.broadcasted_iota(jnp.int32, (rows, columns), 1)
    return jnp.where(row == column, 1.0, 0.0).astype(narrow)


def halves(a, b):
    lane = lax.broadcasted_iota(jnp.int32, (a.shape[0], 128), 1) < 64
    a0, a1, a2 = (a[:, i : i + 128] for i in (0, 128, 256))
    b0, b1, b2 = (b[:, i : i + 128] for i in (0, 128, 256))
    a1_turned, a2_turned, b0_turned, b1_turned = (
        pltpu.roll(v, 64, 1) for v in (a1, a2, b0, b1)
    )
    left = [a0, jnp.where(lane, a1, b0_turned), jnp.where(lane, b0_turned, b1_turned)]
    right = [jnp.where(lane, a1_turned, a2_turned), jnp.where(lane, a2_turned, b1), b2]
    return left, right


def merge_kernel(
    place_ref, own0, own1, far0, far1, x_ref, shift_ref, g_ref, gain_ref, table_ref
):
    blocks, block = own0.shape[0] * own0.shape[1], own0.shape[3]
    rows, half = x_ref.shape[1], block // 2
    first = place_ref[0] == 0

    def sides(own, far):
        a = jnp.where(first, own, far)
        b = jnp.where(first, far, own)
        left = jnp.concatenate([a[:, :half], b[:, :half]], axis=1)
        right = jnp.concatenate([a[:, half:], b[:, half:]], axis=1)
        return left, right

    table_ref[...] = jnp.zeros_like(table_ref)
    for part, (own, far) in enumerate(((own0, far0), (own1, far1))):
        at = slice(part * rows, (part + 1) * rows)
        total = jnp.zeros((rows, 128), wide)
        for index in range(blocks):
            x, j = index % 4, index // 4
            to = slice(index * block, (index + 1) * block)
            values, grads = sides(own[x, j, :rows], far[x, j, :rows])
            x_ref[part, :, to] = values
            wide_to = slice(index % 2 * block, (index % 2 + 1) * block)
            g_ref[index // 2, at, wide_to] = grads
            for lane in range(0, block, 128):
                total = total + values[:, lane : lane + 128].astype(wide)
            if part == 0:
                gain_ref[:, to], _ = sides(own[x, j, rows:].astype(wide), far[x, j, rows:].astype(wide))
        mean = jnp.sum(total, axis=1, keepdims=True) * (1.0 / (blocks * block))
        spread = jnp.zeros((rows, 128), wide)
        for lane in range(0, blocks * block, 128):
            shifted = x_ref[part, :, lane : lane + 128].astype(wide) - mean
            spread = spread + shifted * shifted
            pair, to = lane // (2 * block), lane % (2 * block)
            shift_ref[pair, at, to : to + 128] = (shifted * gain_ref[:1, lane : lane + 128]).astype(narrow)
        columns = split3(mean) + split3(jnp.sum(spread, axis=1, keepdims=True))
        lane = lax.broadcasted_iota(jnp.int32, (rows, 128), 1)
        table = jnp.zeros((rows, 128), wide)
        for index, column in enumerate(columns):
            table = jnp.where(lane == index, column, table)
        table_ref[part, :rows] = table.astype(narrow)


def first_kernel(
    place_ref, gain_ref, table_ref, shift_ref, g_ref, panel_ref, sums0_ref, sums1_ref,
    shift_s, g_s, panel_s, sems,
):
    pairs, tokens, width = shift_ref.shape
    block = width // 2
    flip = place_ref[1]

    def fetch(pair):
        at = (pair // 2 ^ flip) * 2 + pair % 2
        moves = (
            (shift_ref.at[pair], shift_s.at[pair]),
            (g_ref.at[pair], g_s.at[pair]),
            (panel_ref.at[pl.ds(at * 2, 2)], panel_s.at[pair]),
        )
        return [
            pltpu.make_async_copy(source, target, sems.at[pair, i])
            for i, (source, target) in enumerate(moves)
        ]

    for pair in range(pairs):
        for copy in fetch(pair):
            copy.start()

    pre = act = gain_sum = None
    for pair in range(pairs):
        for copy in fetch(pair):
            copy.wait()
        to = slice(pair * width, (pair + 1) * width)
        w_in = panel_s[pair, :, :block].reshape(width, -1)
        w_out = jnp.concatenate([panel_s[pair, i, block:] for i in range(2)], axis=1)
        p = jnp.dot(shift_s[pair], w_in, preferred_element_type=wide)
        a = lax.dot_general(g_s[pair], w_out, (((1,), (1,)), ((), ())), preferred_element_type=wide)
        v = jnp.dot(gain_ref[:, to].astype(narrow), w_in, preferred_element_type=wide)
        pre, act, gain_sum = (p, a, v) if pre is None else (pre + p, act + a, gain_sum + v)

    rows = tokens // 2
    high = gain_sum[:1].astype(narrow).astype(wide)
    for part, sums_ref in enumerate((sums0_ref, sums1_ref)):
        at = slice(part * rows, (part + 1) * rows)
        sums_ref[:rows] = pre[at].astype(narrow)
        sums_ref[rows:tokens] = act[at].astype(narrow)
        lines = lax.dot_general(
            ones_diagonal(16, 128), table_ref[part], (((1,), (1,)), ((), ())), preferred_element_type=wide
        )
        row = lax.broadcasted_iota(jnp.int32, lines.shape, 0)
        lines = jnp.where(row == 6, high, jnp.where(row == 7, gain_sum[:1] - high, lines))
        sums_ref[tokens:] = lines.astype(narrow)


def second_kernel(
    features, part, place_ref, own_ref, far_ref, x_ref, gain_ref, panel_ref, keep_ref, send_ref
):
    rows = x_ref.shape[1]
    blocks, block = panel_ref.shape[0], panel_ref.shape[1] // 2

    def extras(ref):
        lines = ref[2 * rows :]
        table = lax.dot_general(
            lines, ones_diagonal(16, 128), (((0,), (0,)), ((), ())), preferred_element_type=wide
        )[:rows]
        center = table[:, 0:1] + table[:, 1:2] + table[:, 2:3]
        spread = table[:, 3:4] + table[:, 4:5] + table[:, 5:6]
        lines = lines.astype(wide)
        return center, spread, lines[6:7] + lines[7:8]

    mean_a, spread_a, gain_a = extras(own_ref)
    mean_b, spread_b, gain_b = extras(far_ref)
    gap = mean_a - mean_b
    mean = 0.5 * (mean_a + mean_b)
    spread = spread_a + spread_b + gap * gap * (features / 4)
    inverse = lax.rsqrt(spread / features + epsilon)
    total = own_ref[:rows].astype(wide) + far_ref[:rows].astype(wide)
    total = total + (mean_a - mean) * gain_a + (mean_b - mean) * gain_b
    preact = total * inverse
    act_grad = own_ref[rows : 2 * rows].astype(wide) + far_ref[rows : 2 * rows].astype(wide)
    bulk = 0.5 * (1.0 + lax.erf(preact * root_half))
    slope = bulk + preact * jnp.exp(-0.5 * preact * preact) * inv_root_tau
    activation = (preact * bulk).astype(narrow)
    d_pre = (act_grad * slope).astype(narrow)
    d_wide = d_pre.astype(wide)
    flat = inverse * jnp.sum(d_wide * (gain_a + gain_b), axis=1, keepdims=True) / features
    cross = inverse * inverse * jnp.sum(d_wide * preact, axis=1, keepdims=True) / features
    flat = flat - mean * cross

    first = place_ref[0] == 0
    flip = place_ref[1]
    group = 2
    for start in range(0, blocks, group):
        at = (start // 4 ^ flip) * 4 + start % 4
        w_in = panel_ref[pl.ds(at, group), :block].reshape(group * block, -1)
        w_out = jnp.concatenate([panel_ref[at + i, block:] for i in range(group)], axis=1)
        outs = jnp.dot(activation, w_out, preferred_element_type=wide)
        d_normed = lax.dot_general(
            d_pre, w_in, (((1,), (1,)), ((), ())), preferred_element_type=wide
        )
        to = slice(start * block, (start + group) * block)
        grads = inverse * (d_normed * gain_ref[:1, to]) - flat - x_ref[part, :, to].astype(wide) * cross
        for index in range(start, start + group):
            x, j = index % 4, index // 4
            own = slice((index - start) * block, (index - start + 1) * block)
            target = (x - place_ref[2]) & 3 if relative[part] else x
            sides = halves(outs[:, own], grads[:, own])
            for lane in range(3):
                side0, side1 = (side[lane].astype(narrow) for side in sides)
                keep = jnp.where(first, side0, side1)
                send = jnp.where(first, side1, side0)
                to = slice(lane * 128, lane * 128 + 128)
                keep_ref[target, j, :, to] = keep
                send_ref[target, j, :, to] = send


def in_hbm(array):
    return pltpu.with_memory_space_constraint(array, pltpu.HBM)


def call(kernel, in_specs, out_shape, scratch_shapes, vmem, name):
    here = pl.BlockSpec(memory_space=pltpu.VMEM)
    specs = {"scalar": pl.BlockSpec(memory_space=pltpu.SMEM), "here": here, "any": pl.BlockSpec(memory_space=pl.ANY)}
    return pl.pallas_call(
        kernel,
        in_specs=[specs[spec] for spec in in_specs],
        out_specs=[here] * len(out_shape),
        out_shape=out_shape,
        scratch_shapes=scratch_shapes,
        compiler_params=pltpu.CompilerParams(vmem_limit_bytes=vmem * 2**20),
        name=name,
    )


def merge_call(place, own0, own1, far0, far1, hidden):
    blocks, block = own0.shape[0] * own0.shape[1], own0.shape[3]
    tokens, width = 2 * (own0.shape[2] - 8), blocks * block
    return call(
        merge_kernel,
        ["scalar", "here", "here", "here", "here"],
        [
            pltpu.HBM((2, tokens // 2, width), narrow),
            pltpu.HBM((blocks // 2, tokens, 2 * block), narrow),
            pltpu.HBM((blocks // 2, tokens, 2 * block), narrow),
            jax.ShapeDtypeStruct((8, width), wide),
            jax.ShapeDtypeStruct((2, hidden, 128), narrow),
        ],
        [],
        30,
        "merge",
    )(place, own0, own1, far0, far1)


def first_call(place, shifted, grads, gains, table, panels):
    blocks, twice, hidden = panels.shape
    pairs, tokens, width = shifted.shape
    sums = jax.ShapeDtypeStruct((tokens + 16, hidden), narrow)
    return call(
        first_kernel,
        ["scalar", "here", "here", "any", "any", "any"],
        [sums, sums],
        [
            pltpu.VMEM(shifted.shape, narrow),
            pltpu.VMEM(grads.shape, narrow),
            pltpu.VMEM((pairs, blocks // pairs, twice, hidden), narrow),
            pltpu.SemaphoreType.DMA((pairs, 3)),
        ],
        30,
        "first",
    )(place, gains, table, in_hbm(shifted), in_hbm(grads), in_hbm(panels))


def second_call(features, part, place, sums, far_sums, values, gains, panels):
    out = jax.ShapeDtypeStruct((4, 2, values.shape[1], panels.shape[1] // 2), narrow)
    return call(
        functools.partial(second_kernel, features, part),
        ["scalar", "here", "here", "here", "here", "here"],
        [out, out],
        [],
        30,
        "second",
    )(place, sums, far_sums, values, gains, panels)


def on_device(inputs, gain, w_in, w_out, grad_out):
    rows, piece = inputs.shape
    block = 2 * piece
    features = piece * lax.axis_size(("h", "x", "k"))
    other_core = [(0, 1), (1, 0)]
    place = jnp.stack([lax.axis_index("k"), lax.axis_index("h") % 2, lax.axis_index("x")]).astype(jnp.int32)

    panels = lax.all_gather(jnp.concatenate([w_in, w_out], axis=0), "y", axis=0)

    gain_rows = jnp.broadcast_to(jnp.concatenate([gain, gain])[None, :], (8, block))
    pack = jnp.concatenate([jnp.concatenate([inputs, grad_out], axis=1), gain_rows], axis=0)
    near = [
        [lax.ppermute(pack, ("l", "h"), gather_pairs(i, j)) for j in range(2)] for i in range(2)
    ]
    own0 = lax.all_gather(jnp.stack(near[0]), "x", axis=0)
    far0 = lax.ppermute(own0, "k", other_core)
    own1 = lax.all_gather(jnp.stack(near[1]), "x", axis=0)
    far1 = lax.ppermute(own1, "k", other_core)

    values, shifted, grads, gains, table = merge_call(place, own0, own1, far0, far1, w_in.shape[1])
    sums = first_call(place, shifted, grads, gains, table, panels)
    far_sums = [lax.ppermute(part, "l", other_core) for part in sums]
    keep, got = [], []
    for i in range(2):
        kept, send = second_call(features, i, place, sums[i], far_sums[i], values, gains, panels)
        keep.append(kept)
        got.append(lax.ppermute(send, "k", other_core))

    def add(a, b):
        return (a.astype(wide) + b.astype(wide)).astype(narrow)

    shares = []
    for i in range(2):
        if relative[i]:
            parts = [add(keep[i][d], got[i][d]) for d in range(4)]
            parts = [parts[0]] + [
                lax.ppermute(parts[d], "x", [(x, (x + d) % 4) for x in range(4)]) for d in (1, 3, 2)
            ]
        else:
            parts = lax.all_to_all(add(keep[i], got[i]), "x", 0, 0)
            parts = [parts[x] for x in range(4)]
        part = sum(part.astype(wide) for part in parts).astype(narrow)
        shares += [lax.ppermute(part[j], ("l", "h"), scatter_pairs(i, j)).astype(wide) for j in range(2)]
    total = (shares[0] + shares[1] + shares[2] + shares[3]).astype(narrow)
    return (total[:, :piece], total[:, piece:])


def solution(mesh):
    fine = Mesh(mesh.devices.reshape(2, 8, 4, 4, 2), ("l", "y", "h", "x", "k"))
    row, col = ("l", "y"), ("h", "x", "k")
    in_specs = (P(row, col), P(col), P(row, col), P(col, row), P(row, col))
    out_specs = (P(row, col), P(row, col))
    return jax.shard_map(
        on_device, mesh=fine, in_specs=in_specs, out_specs=out_specs, check_vma=False
    )
```

```python
import functools

import jax
import jax.numpy as jnp
from jax import lax
from jax.experimental import pallas as pl
from jax.experimental.pallas import tpu as pltpu
from jax.sharding import Mesh
from jax.sharding import PartitionSpec as P

root_half = 0.7071067811865476
inv_root_tau = 0.3989422804014327
epsilon = 1e-06
narrow = jnp.bfloat16
wide = jnp.float32

def pairs_of(target):
    pairs = []
    for l in range(2):
        for h in range(4):
            new_l, new_high, new_low = target(l, h // 2, h % 2)
            pairs.append((l * 4 + h, new_l * 4 + new_high * 2 + new_low))
    return pairs


def gather_pairs(i, j):
    return pairs_of(lambda l, high, low: (high, l ^ i, low ^ j))


def scatter_pairs(i, j):
    return pairs_of(lambda l, high, low: (high ^ i, l, low ^ j))


def split3(value):
    high = value.astype(narrow).astype(wide)
    middle = (value - high).astype(narrow).astype(wide)
    return high, middle, value - high - middle


def ones_diagonal(rows, columns):
    row = lax.broadcasted_iota(jnp.int32, (rows, columns), 0)
    column = lax.broadcasted_iota(jnp.int32, (rows, columns), 1)
    return jnp.where(row == column, 1.0, 0.0).astype(narrow)


def halves(a, b):
    lane = lax.broadcasted_iota(jnp.int32, (a.shape[0], 128), 1) < 64
    a0, a1, a2 = (a[:, i : i + 128] for i in (0, 128, 256))
    b0, b1, b2 = (b[:, i : i + 128] for i in (0, 128, 256))
    a1_turned, a2_turned, b0_turned, b1_turned = (
        pltpu.roll(v, 64, 1) for v in (a1, a2, b0, b1)
    )
    left = [a0, jnp.where(lane, a1, b0_turned), jnp.where(lane, b0_turned, b1_turned)]
    right = [jnp.where(lane, a1_turned, a2_turned), jnp.where(lane, a2_turned, b1), b2]
    return left, right


def merge_kernel(
    place_ref, own0, own1, far0, far1, x_ref, shift_ref, g_ref, gain_ref, table_ref
):
    blocks, block = own0.shape[0] * own0.shape[1], own0.shape[3]
    rows, half = x_ref.shape[1], block // 2
    first = place_ref[0] == 0

    def sides(own, far):
        a = jnp.where(first, own, far)
        b = jnp.where(first, far, own)
        left = jnp.concatenate([a[:, :half], b[:, :half]], axis=1)
        right = jnp.concatenate([a[:, half:], b[:, half:]], axis=1)
        return left, right

    table_ref[...] = jnp.zeros_like(table_ref)
    for part, (own, far) in enumerate(((own0, far0), (own1, far1))):
        total = jnp.zeros((rows, 128), wide)
        for index in range(blocks):
            x, j = index % 4, index // 4
            to = slice(index * block, (index + 1) * block)
            values, grads = sides(own[x, j, :rows], far[x, j, :rows])
            x_ref[part, :, to] = values
            wide_to = slice(index % 2 * block, (index % 2 + 1) * block)
            g_ref[part, index // 2, :, wide_to] = grads
            for lane in range(0, block, 128):
                total = total + values[:, lane : lane + 128].astype(wide)
            if part == 0:
                gain_ref[:, to], _ = sides(own[x, j, rows:].astype(wide), far[x, j, rows:].astype(wide))
        mean = jnp.sum(total, axis=1, keepdims=True) * (1.0 / (blocks * block))
        spread = jnp.zeros((rows, 128), wide)
        for lane in range(0, blocks * block, 128):
            shifted = x_ref[part, :, lane : lane + 128].astype(wide) - mean
            spread = spread + shifted * shifted
            pair, to = lane // (2 * block), lane % (2 * block)
            shift_ref[part, pair, :, to : to + 128] = (shifted * gain_ref[:1, lane : lane + 128]).astype(narrow)
        columns = split3(mean) + split3(jnp.sum(spread, axis=1, keepdims=True))
        lane = lax.broadcasted_iota(jnp.int32, (rows, 128), 1)
        table = jnp.zeros((rows, 128), wide)
        for index, column in enumerate(columns):
            table = jnp.where(lane == index, column, table)
        table_ref[part, :rows] = table.astype(narrow)


def first_kernel(
    part, place_ref, gain_ref, table_ref, shift_ref, g_ref, panel_ref, sums_ref,
    shift_s, g_s, panel_s, sems,
):
    pairs, rows, width = shift_s.shape
    block = width // 2
    flip = place_ref[1]

    def panels_at(pair):
        return panel_ref.at[pl.ds(((pair // 2 ^ flip) * 2 + pair % 2) * 2, 2)]

    def fetch(pair):
        moves = [(shift_ref.at[part, pair], shift_s.at[pair]), (g_ref.at[part, pair], g_s.at[pair])]
        if part == 0:
            moves.append((panels_at(pair), panel_s.at[pair]))
        return [
            pltpu.make_async_copy(source, target, sems.at[pair, i])
            for i, (source, target) in enumerate(moves)
        ]

    for pair in range(pairs):
        for copy in fetch(pair):
            copy.start()

    pre = act = gain_sum = None
    for pair in range(pairs):
        for copy in fetch(pair):
            copy.wait()
        to = slice(pair * width, (pair + 1) * width)
        panel = panel_s[pair] if part == 0 else panels_at(pair)[...]
        w_in = panel[:, :block].reshape(width, -1)
        w_out = jnp.concatenate([panel[i, block:] for i in range(2)], axis=1)
        p = jnp.dot(shift_s[pair], w_in, preferred_element_type=wide)
        a = lax.dot_general(g_s[pair], w_out, (((1,), (1,)), ((), ())), preferred_element_type=wide)
        v = jnp.dot(gain_ref[:, to].astype(narrow), w_in, preferred_element_type=wide)
        pre, act, gain_sum = (p, a, v) if pre is None else (pre + p, act + a, gain_sum + v)

    sums_ref[:rows] = pre.astype(narrow)
    sums_ref[rows : 2 * rows] = act.astype(narrow)
    lines = lax.dot_general(
        ones_diagonal(16, 128), table_ref[part], (((1,), (1,)), ((), ())), preferred_element_type=wide
    )
    high = gain_sum[:1].astype(narrow).astype(wide)
    row = lax.broadcasted_iota(jnp.int32, lines.shape, 0)
    lines = jnp.where(row == 6, high, jnp.where(row == 7, gain_sum[:1] - high, lines))
    sums_ref[2 * rows :] = lines.astype(narrow)


def second_kernel(
    features, part, place_ref, own_ref, far_ref, x_ref, gain_ref, panel_ref, keep_ref, send_ref
):
    rows = x_ref.shape[1]
    blocks, block = panel_ref.shape[0], panel_ref.shape[1] // 2

    def extras(ref):
        lines = ref[2 * rows :]
        table = lax.dot_general(
            lines, ones_diagonal(16, 128), (((0,), (0,)), ((), ())), preferred_element_type=wide
        )[:rows]
        center = table[:, 0:1] + table[:, 1:2] + table[:, 2:3]
        spread = table[:, 3:4] + table[:, 4:5] + table[:, 5:6]
        lines = lines.astype(wide)
        return center, spread, lines[6:7] + lines[7:8]

    mean_a, spread_a, gain_a = extras(own_ref)
    mean_b, spread_b, gain_b = extras(far_ref)
    gap = mean_a - mean_b
    mean = 0.5 * (mean_a + mean_b)
    spread = spread_a + spread_b + gap * gap * (features / 4)
    inverse = lax.rsqrt(spread / features + epsilon)
    total = own_ref[:rows].astype(wide) + far_ref[:rows].astype(wide)
    total = total + (mean_a - mean) * gain_a + (mean_b - mean) * gain_b
    preact = total * inverse
    act_grad = own_ref[rows : 2 * rows].astype(wide) + far_ref[rows : 2 * rows].astype(wide)
    bulk = 0.5 * (1.0 + lax.erf(preact * root_half))
    slope = bulk + preact * jnp.exp(-0.5 * preact * preact) * inv_root_tau
    activation = (preact * bulk).astype(narrow)
    d_pre = (act_grad * slope).astype(narrow)
    d_wide = d_pre.astype(wide)
    flat = inverse * jnp.sum(d_wide * (gain_a + gain_b), axis=1, keepdims=True) / features
    cross = inverse * inverse * jnp.sum(d_wide * preact, axis=1, keepdims=True) / features
    flat = flat - mean * cross

    first = place_ref[0] == 0
    flip = place_ref[1]
    group = 2
    for start in range(0, blocks, group):
        at = (start // 4 ^ flip) * 4 + start % 4
        w_in = panel_ref[pl.ds(at, group), :block].reshape(group * block, -1)
        w_out = jnp.concatenate([panel_ref[at + i, block:] for i in range(group)], axis=1)
        outs = jnp.dot(activation, w_out, preferred_element_type=wide)
        d_normed = lax.dot_general(
            d_pre, w_in, (((1,), (1,)), ((), ())), preferred_element_type=wide
        )
        to = slice(start * block, (start + group) * block)
        grads = inverse * (d_normed * gain_ref[:1, to]) - flat - x_ref[part, :, to].astype(wide) * cross
        for index in range(start, start + group):
            x, j = index % 4, index // 4
            own = slice((index - start) * block, (index - start + 1) * block)
            target = (x - place_ref[2]) & 3
            sides = halves(outs[:, own], grads[:, own])
            for lane in range(3):
                side0, side1 = (side[lane].astype(narrow) for side in sides)
                keep = jnp.where(first, side0, side1)
                send = jnp.where(first, side1, side0)
                to = slice(lane * 128, lane * 128 + 128)
                keep_ref[target, j, :, to] = keep
                send_ref[target, j, :, to] = send


def in_hbm(array):
    return pltpu.with_memory_space_constraint(array, pltpu.HBM)


def call(kernel, in_specs, out_shape, scratch_shapes, vmem, name):
    here = pl.BlockSpec(memory_space=pltpu.VMEM)
    specs = {"scalar": pl.BlockSpec(memory_space=pltpu.SMEM), "here": here, "any": pl.BlockSpec(memory_space=pl.ANY)}
    return pl.pallas_call(
        kernel,
        in_specs=[specs[spec] for spec in in_specs],
        out_specs=[here] * len(out_shape),
        out_shape=out_shape,
        scratch_shapes=scratch_shapes,
        compiler_params=pltpu.CompilerParams(vmem_limit_bytes=vmem * 2**20),
        name=name,
    )


def merge_call(place, own0, own1, far0, far1, hidden):
    blocks, block = own0.shape[0] * own0.shape[1], own0.shape[3]
    tokens, width = 2 * (own0.shape[2] - 8), blocks * block
    return call(
        merge_kernel,
        ["scalar", "here", "here", "here", "here"],
        [
            pltpu.HBM((2, tokens // 2, width), narrow),
            pltpu.HBM((2, blocks // 2, tokens // 2, 2 * block), narrow),
            pltpu.HBM((2, blocks // 2, tokens // 2, 2 * block), narrow),
            jax.ShapeDtypeStruct((8, width), wide),
            jax.ShapeDtypeStruct((2, hidden, 128), narrow),
        ],
        [],
        30,
        "merge",
    )(place, own0, own1, far0, far1)


def first_call(part, place, shifted, grads, gains, table, panels):
    blocks, twice, hidden = panels.shape
    _, pairs, rows, width = shifted.shape
    panel_copy = (pairs, blocks // pairs, twice, hidden) if part == 0 else (1, 16, 128)
    (sums,) = call(
        functools.partial(first_kernel, part),
        ["scalar", "here", "here", "any", "any", "here" if part else "any"],
        [jax.ShapeDtypeStruct((2 * rows + 16, hidden), narrow)],
        [
            pltpu.VMEM((pairs, rows, width), narrow),
            pltpu.VMEM((pairs, rows, width), narrow),
            pltpu.VMEM(panel_copy, narrow),
            pltpu.SemaphoreType.DMA((pairs, 3)),
        ],
        30,
        "first",
    )(place, gains, table, in_hbm(shifted), in_hbm(grads), panels if part else in_hbm(panels))
    return sums


def second_call(features, part, place, sums, far_sums, values, gains, panels):
    out = jax.ShapeDtypeStruct((4, 2, values.shape[1], panels.shape[1] // 2), narrow)
    return call(
        functools.partial(second_kernel, features, part),
        ["scalar", "here", "here", "here", "here", "here"],
        [out, out],
        [],
        30,
        "second",
    )(place, sums, far_sums, values, gains, panels)


def on_device(inputs, gain, w_in, w_out, grad_out):
    rows, piece = inputs.shape
    block = 2 * piece
    features = piece * lax.axis_size(("h", "x", "k"))
    other_core = [(0, 1), (1, 0)]
    place = jnp.stack([lax.axis_index("k"), lax.axis_index("h") % 2, lax.axis_index("x")]).astype(jnp.int32)

    panels = lax.all_gather(jnp.concatenate([w_in, w_out], axis=0), "y", axis=0)

    gain_rows = jnp.broadcast_to(jnp.concatenate([gain, gain])[None, :], (8, block))
    pack = jnp.concatenate([jnp.concatenate([inputs, grad_out], axis=1), gain_rows], axis=0)
    near = [
        [lax.ppermute(pack, ("l", "h"), gather_pairs(i, j)) for j in range(2)] for i in range(2)
    ]
    own0 = lax.all_gather(jnp.stack(near[0]), "x", axis=0)
    far0 = lax.ppermute(own0, "k", other_core)
    own1 = lax.all_gather(jnp.stack(near[1]), "x", axis=0)
    far1 = lax.ppermute(own1, "k", other_core)

    values, shifted, grads, gains, table = merge_call(place, own0, own1, far0, far1, w_in.shape[1])
    sums = [first_call(i, place, shifted, grads, gains, table, panels) for i in range(2)]
    far_sums = [lax.ppermute(part, "l", other_core) for part in sums]
    keep, got = [], []
    for i in range(2):
        kept, send = second_call(features, i, place, sums[i], far_sums[i], values, gains, panels)
        keep.append(kept)
        got.append(lax.ppermute(send, "k", other_core))

    def add(a, b):
        return (a.astype(wide) + b.astype(wide)).astype(narrow)

    shares = []
    for i in range(2):
        parts = [add(keep[i][d], got[i][d]) for d in range(4)]
        parts = [parts[0]] + [
            lax.ppermute(parts[d], "x", [(x, (x + d) % 4) for x in range(4)]) for d in (3, 1, 2)
        ]
        part = sum(part.astype(wide) for part in parts).astype(narrow)
        shares += [lax.ppermute(part[j], ("l", "h"), scatter_pairs(i, j)).astype(wide) for j in range(2)]
    total = (shares[0] + shares[1] + shares[2] + shares[3]).astype(narrow)
    return (total[:, :piece], total[:, piece:])


def solution(mesh):
    fine = Mesh(mesh.devices.reshape(2, 8, 4, 4, 2), ("l", "y", "h", "x", "k"))
    row, col = ("l", "y"), ("h", "x", "k")
    in_specs = (P(row, col), P(col), P(row, col), P(col, row), P(row, col))
    out_specs = (P(row, col), P(row, col))
    return jax.shard_map(
        on_device, mesh=fine, in_specs=in_specs, out_specs=out_specs, check_vma=False
    )
```

```python
import functools

import jax
import jax.numpy as jnp
from jax import lax
from jax.experimental import pallas as pl
from jax.experimental.pallas import tpu as pltpu
from jax.sharding import Mesh
from jax.sharding import PartitionSpec as P

root_half = 0.7071067811865476
inv_root_tau = 0.3989422804014327
epsilon = 1e-06
narrow = jnp.bfloat16
wide = jnp.float32

def pairs_of(target):
    pairs = []
    for l in range(2):
        for h in range(4):
            new_l, new_high, new_low = target(l, h // 2, h % 2)
            pairs.append((l * 4 + h, new_l * 4 + new_high * 2 + new_low))
    return pairs


def gather_pairs(i, j):
    return pairs_of(lambda l, high, low: (high, l ^ i, low ^ j))


def scatter_pairs(i, j):
    return pairs_of(lambda l, high, low: (high ^ i, l, low ^ j))


def split3(value):
    high = value.astype(narrow).astype(wide)
    middle = (value - high).astype(narrow).astype(wide)
    return high, middle, value - high - middle


def ones_diagonal(rows, columns):
    row = lax.broadcasted_iota(jnp.int32, (rows, columns), 0)
    column = lax.broadcasted_iota(jnp.int32, (rows, columns), 1)
    return jnp.where(row == column, 1.0, 0.0).astype(narrow)


def halves(a, b):
    lane = lax.broadcasted_iota(jnp.int32, (a.shape[0], 128), 1) < 64
    a0, a1, a2 = (a[:, i : i + 128] for i in (0, 128, 256))
    b0, b1, b2 = (b[:, i : i + 128] for i in (0, 128, 256))
    a1_turned, a2_turned, b0_turned, b1_turned = (
        pltpu.roll(v, 64, 1) for v in (a1, a2, b0, b1)
    )
    left = [a0, jnp.where(lane, a1, b0_turned), jnp.where(lane, b0_turned, b1_turned)]
    right = [jnp.where(lane, a1_turned, a2_turned), jnp.where(lane, a2_turned, b1), b2]
    return left, right


def merge_kernel(
    place_ref, own0, own1, far0, far1, x_ref, shift_ref, g_ref, gain_ref, table_ref
):
    blocks, block = own0.shape[0] * own0.shape[1], own0.shape[3]
    rows, half = x_ref.shape[1], block // 2
    first = place_ref[0] == 0

    def sides(own, far):
        a = jnp.where(first, own, far)
        b = jnp.where(first, far, own)
        left = jnp.concatenate([a[:, :half], b[:, :half]], axis=1)
        right = jnp.concatenate([a[:, half:], b[:, half:]], axis=1)
        return left, right

    table_ref[...] = jnp.zeros_like(table_ref)
    for part, (own, far) in enumerate(((own0, far0), (own1, far1))):
        total = jnp.zeros((rows, 128), wide)
        for index in range(blocks):
            x, j = index % 4, index // 4
            to = slice(index * block, (index + 1) * block)
            values, grads = sides(own[x, j, :rows], far[x, j, :rows])
            x_ref[part, :, to] = values
            wide_to = slice(index % 2 * block, (index % 2 + 1) * block)
            g_ref[part, index // 2, :, wide_to] = grads
            for lane in range(0, block, 128):
                total = total + values[:, lane : lane + 128].astype(wide)
            if part == 0:
                gain_ref[:, to], _ = sides(own[x, j, rows:].astype(wide), far[x, j, rows:].astype(wide))
        mean = jnp.sum(total, axis=1, keepdims=True) * (1.0 / (blocks * block))
        spread = jnp.zeros((rows, 128), wide)
        for lane in range(0, blocks * block, 128):
            shifted = x_ref[part, :, lane : lane + 128].astype(wide) - mean
            spread = spread + shifted * shifted
            pair, to = lane // (2 * block), lane % (2 * block)
            shift_ref[part, pair, :, to : to + 128] = (shifted * gain_ref[:1, lane : lane + 128]).astype(narrow)
        columns = split3(mean) + split3(jnp.sum(spread, axis=1, keepdims=True))
        lane = lax.broadcasted_iota(jnp.int32, (rows, 128), 1)
        table = jnp.zeros((rows, 128), wide)
        for index, column in enumerate(columns):
            table = jnp.where(lane == index, column, table)
        table_ref[part, :rows] = table.astype(narrow)


def first_kernel(
    part, place_ref, gain_ref, table_ref, shift_ref, g_ref, panel_ref, sums_ref,
    shift_s, g_s, panel_s, sems,
):
    pairs, rows, width = shift_s.shape
    block = width // 2
    flip = place_ref[1]

    def panels_at(pair):
        return panel_ref.at[pl.ds(((pair // 2 ^ flip) * 2 + pair % 2) * 2, 2)]

    def fetch(pair):
        moves = [(shift_ref.at[part, pair], shift_s.at[pair]), (g_ref.at[part, pair], g_s.at[pair])]
        if part == 0:
            moves.append((panels_at(pair), panel_s.at[pair]))
        return [
            pltpu.make_async_copy(source, target, sems.at[pair, i])
            for i, (source, target) in enumerate(moves)
        ]

    for pair in range(pairs):
        for copy in fetch(pair):
            copy.start()

    pre = act = gain_sum = None
    for pair in range(pairs):
        for copy in fetch(pair):
            copy.wait()
        to = slice(pair * width, (pair + 1) * width)
        panel = panel_s[pair] if part == 0 else panels_at(pair)[...]
        w_in = panel[:, :block].reshape(width, -1)
        w_out = jnp.concatenate([panel[i, block:] for i in range(2)], axis=1)
        p = jnp.dot(shift_s[pair], w_in, preferred_element_type=wide)
        a = lax.dot_general(g_s[pair], w_out, (((1,), (1,)), ((), ())), preferred_element_type=wide)
        v = jnp.dot(gain_ref[:, to].astype(narrow), w_in, preferred_element_type=wide)
        pre, act, gain_sum = (p, a, v) if pre is None else (pre + p, act + a, gain_sum + v)

    sums_ref[:rows] = pre.astype(narrow)
    sums_ref[rows : 2 * rows] = act.astype(narrow)
    lines = lax.dot_general(
        ones_diagonal(16, 128), table_ref[part], (((1,), (1,)), ((), ())), preferred_element_type=wide
    )
    high = gain_sum[:1].astype(narrow).astype(wide)
    row = lax.broadcasted_iota(jnp.int32, lines.shape, 0)
    lines = jnp.where(row == 6, high, jnp.where(row == 7, gain_sum[:1] - high, lines))
    sums_ref[2 * rows :] = lines.astype(narrow)


def second_kernel(
    features, part, place_ref, own_ref, far_ref, x_ref, gain_ref, panel_ref, keep_ref, send_ref
):
    rows = x_ref.shape[1]
    blocks, block = panel_ref.shape[0], panel_ref.shape[1] // 2

    def extras(ref):
        lines = ref[2 * rows :]
        table = lax.dot_general(
            lines, ones_diagonal(16, 128), (((0,), (0,)), ((), ())), preferred_element_type=wide
        )[:rows]
        center = table[:, 0:1] + table[:, 1:2] + table[:, 2:3]
        spread = table[:, 3:4] + table[:, 4:5] + table[:, 5:6]
        lines = lines.astype(wide)
        return center, spread, lines[6:7] + lines[7:8]

    mean_a, spread_a, gain_a = extras(own_ref)
    mean_b, spread_b, gain_b = extras(far_ref)
    gap = mean_a - mean_b
    mean = 0.5 * (mean_a + mean_b)
    spread = spread_a + spread_b + gap * gap * (features / 4)
    inverse = lax.rsqrt(spread / features + epsilon)
    total = own_ref[:rows].astype(wide) + far_ref[:rows].astype(wide)
    total = total + (mean_a - mean) * gain_a + (mean_b - mean) * gain_b
    preact = total * inverse
    act_grad = own_ref[rows : 2 * rows].astype(wide) + far_ref[rows : 2 * rows].astype(wide)
    bulk = 0.5 * (1.0 + lax.erf(preact * root_half))
    slope = bulk + preact * jnp.exp(-0.5 * preact * preact) * inv_root_tau
    activation = (preact * bulk).astype(narrow)
    d_pre = (act_grad * slope).astype(narrow)
    d_wide = d_pre.astype(wide)
    flat = inverse * jnp.sum(d_wide * (gain_a + gain_b), axis=1, keepdims=True) / features
    cross = inverse * inverse * jnp.sum(d_wide * preact, axis=1, keepdims=True) / features
    flat = flat - mean * cross

    first = place_ref[0] == 0
    flip = place_ref[1]
    group = 2
    for start in range(0, blocks, group):
        at = (start // 4 ^ flip) * 4 + start % 4
        w_in = panel_ref[pl.ds(at, group), :block].reshape(group * block, -1)
        w_out = jnp.concatenate([panel_ref[at + i, block:] for i in range(group)], axis=1)
        outs = jnp.dot(activation, w_out, preferred_element_type=wide)
        d_normed = lax.dot_general(
            d_pre, w_in, (((1,), (1,)), ((), ())), preferred_element_type=wide
        )
        to = slice(start * block, (start + group) * block)
        grads = inverse * (d_normed * gain_ref[:1, to]) - flat - x_ref[part, :, to].astype(wide) * cross
        for index in range(start, start + group):
            x, j = index % 4, index // 4
            own = slice((index - start) * block, (index - start + 1) * block)
            target = (x - place_ref[2]) & 3
            sides = halves(outs[:, own], grads[:, own])
            for lane in range(3):
                side0, side1 = (side[lane].astype(narrow) for side in sides)
                keep = jnp.where(first, side0, side1)
                send = jnp.where(first, side1, side0)
                to = slice(lane * 128, lane * 128 + 128)
                keep_ref[target, j, :, to] = keep
                send_ref[target, j, :, to] = send


def in_hbm(array):
    return pltpu.with_memory_space_constraint(array, pltpu.HBM)


def call(kernel, in_specs, out_shape, scratch_shapes, vmem, name):
    here = pl.BlockSpec(memory_space=pltpu.VMEM)
    specs = {"scalar": pl.BlockSpec(memory_space=pltpu.SMEM), "here": here, "any": pl.BlockSpec(memory_space=pl.ANY)}
    return pl.pallas_call(
        kernel,
        in_specs=[specs[spec] for spec in in_specs],
        out_specs=[here] * len(out_shape),
        out_shape=out_shape,
        scratch_shapes=scratch_shapes,
        compiler_params=pltpu.CompilerParams(vmem_limit_bytes=vmem * 2**20),
        name=name,
    )


def merge_call(place, own0, own1, far0, far1, hidden):
    blocks, block = own0.shape[0] * own0.shape[1], own0.shape[3]
    tokens, width = 2 * (own0.shape[2] - 8), blocks * block
    return call(
        merge_kernel,
        ["scalar", "here", "here", "here", "here"],
        [
            pltpu.HBM((2, tokens // 2, width), narrow),
            pltpu.HBM((2, blocks // 2, tokens // 2, 2 * block), narrow),
            pltpu.HBM((2, blocks // 2, tokens // 2, 2 * block), narrow),
            jax.ShapeDtypeStruct((8, width), wide),
            jax.ShapeDtypeStruct((2, hidden, 128), narrow),
        ],
        [],
        30,
        "merge",
    )(place, own0, own1, far0, far1)


def first_call(part, place, shifted, grads, gains, table, panels):
    blocks, twice, hidden = panels.shape
    _, pairs, rows, width = shifted.shape
    panel_copy = (pairs, blocks // pairs, twice, hidden) if part == 0 else (1, 16, 128)
    (sums,) = call(
        functools.partial(first_kernel, part),
        ["scalar", "here", "here", "any", "any", "here" if part else "any"],
        [jax.ShapeDtypeStruct((2 * rows + 16, hidden), narrow)],
        [
            pltpu.VMEM((pairs, rows, width), narrow),
            pltpu.VMEM((pairs, rows, width), narrow),
            pltpu.VMEM(panel_copy, narrow),
            pltpu.SemaphoreType.DMA((pairs, 3)),
        ],
        30,
        "first",
    )(place, gains, table, in_hbm(shifted), in_hbm(grads), panels if part else in_hbm(panels))
    return sums


def second_call(features, part, place, sums, far_sums, values, gains, panels):
    out = jax.ShapeDtypeStruct((4, 2, values.shape[1], panels.shape[1] // 2), narrow)
    return call(
        functools.partial(second_kernel, features, part),
        ["scalar", "here", "here", "here", "here", "here"],
        [out, out],
        [],
        30,
        "second",
    )(place, sums, far_sums, values, gains, panels)


def on_device(inputs, gain, w_in, w_out, grad_out):
    rows, piece = inputs.shape
    block = 2 * piece
    features = piece * lax.axis_size(("h", "x", "k"))
    other_core = [(0, 1), (1, 0)]
    place = jnp.stack([lax.axis_index("k"), lax.axis_index("h") % 2, lax.axis_index("x")]).astype(jnp.int32)

    panels = lax.all_gather(jnp.concatenate([w_in, w_out], axis=0), "y", axis=0)

    gain_rows = jnp.broadcast_to(jnp.concatenate([gain, gain])[None, :], (8, block))
    pack = jnp.concatenate([jnp.concatenate([inputs, grad_out], axis=1), gain_rows], axis=0)
    near = [
        [lax.ppermute(pack, ("l", "h"), gather_pairs(i, j)) for j in range(2)] for i in range(2)
    ]
    own0 = lax.all_gather(jnp.stack(near[0]), "x", axis=0)
    far0 = lax.ppermute(own0, "k", other_core)
    own1 = lax.all_gather(jnp.stack(near[1]), "x", axis=0)
    far1 = lax.ppermute(own1, "k", other_core)

    values, shifted, grads, gains, table = merge_call(place, own0, own1, far0, far1, w_in.shape[1])
    sums = [first_call(i, place, shifted, grads, gains, table, panels) for i in range(2)]
    far_sums = [lax.ppermute(part, "l", other_core) for part in sums]
    keep, got = [], []
    for i in range(2):
        kept, send = second_call(features, i, place, sums[i], far_sums[i], values, gains, panels)
        keep.append(kept)
        got.append(lax.ppermute(send, "k", other_core))

    def add(a, b):
        return (a.astype(wide) + b.astype(wide)).astype(narrow)

    shares = []
    for i in range(2):
        parts = [add(keep[i][d], got[i][d]) for d in range(4)]
        parts = [parts[0]] + [
            lax.ppermute(parts[d], "x", [(x, (x + d) % 4) for x in range(4)]) for d in (3, 1, 2)
        ]
        part = sum(part.astype(wide) for part in parts).astype(narrow)
        shares += [lax.ppermute(part[j], ("l", "h"), scatter_pairs(i, j)).astype(wide) for j in (1, 0)]
    total = (shares[0] + shares[1] + shares[2] + shares[3]).astype(narrow)
    return (total[:, :piece], total[:, piece:])


def solution(mesh):
    fine = Mesh(mesh.devices.reshape(2, 8, 4, 4, 2), ("l", "y", "h", "x", "k"))
    row, col = ("l", "y"), ("h", "x", "k")
    in_specs = (P(row, col), P(col), P(row, col), P(col, row), P(row, col))
    out_specs = (P(row, col), P(row, col))
    return jax.shard_map(
        on_device, mesh=fine, in_specs=in_specs, out_specs=out_specs, check_vma=False
    )
```
